512 devices in a mesh: gx: 16 (over y, x), gy: 32 (over z, core).
Axes of the slice: x: 4, y: 4, z: 16, core: 2. Of those that a mesh axis runs over, the one named last changes fastest.
Arguments:
- points: float32 [3, 1048576], P(None, ('gx', 'gy')), as said below
- targets: float32 [64, 1048576], P(None, ('gx', 'gy')), may hold values from -6 to 6
- basis: float32 [2048, 64, 512], P(('gx', 'gy')), may hold values from -0.25 to 0.25
- leaf_transfer: float32 [2048, 64, 64], P(('gx', 'gy')), may hold values from -0.75 to 0.75
- cell_transfer: float32 [512, 64, 64], P(('gx', 'gy')), may hold values from -0.75 to 0.75
- box_parent_transfer: float32 [16, 64, 64], replicated, may hold values from -0.75 to 0.75
- cell_coupling: float32 [512, 4, 64, 64], P(('gx', 'gy')), as said below
- box_coupling: float32 [16, 3, 64, 64], replicated, as said below
- top_coupling: float32 [8, 4, 64, 64], replicated, as said below
- neighbours: int32 [2048, 6], P(('gx', 'gy')), may hold values from 0 to 2047, as said below
- cell_lists: int32 [512, 4], P(('gx', 'gy')), may hold values from 0 to 511, as said below
Outputs:
- solution: float32 [64, 1048576], P(None, ('gx', 'gy'))
- residual: float32 [64, 1048576], P(None, ('gx', 'gy'))
The draws below stay inside these ranges and needn't reach their ends.
Inputs may be any that keep to these rules, and one draw needn't show every extreme that they name: Leaf i's points lie in the unit cell whose corner is the grid position decoded from i's Morton code. `neighbours`: row i is i, i ^ 4, then i ^ m for 4 distinct masks m among 1, 2, 3, 5, 6, 7 (^ is bitwise exclusive or), the same masks in the same order for all leaves of a block of 8 leaves (the same i // 8); so j stands in row i exactly when i stands in row j, and their cells touch. `cell_lists`: the boxes of each second-level box carry a numbering 0 to 31; entry s of row b is the box of b's second-level box whose number is b's number ^ m_s, with 4 distinct nonzero masks m_s common to that second-level box; so b' stands at position s of row b exactly when b stands at position s of row b'. cell_coupling[b', s] is the transpose of cell_coupling[b, s] where b' = cell_lists[b, s]. box_coupling[g ^ (s + 1), s] is the transpose of box_coupling[g, s]. top_coupling[t ^ (s + 1), s] is the transpose of top_coupling[t, s].
All inputs are finite; a program needn't handle non-finite values.
Results may differ from the reference program's by a relative error of at most 0.0014.
Values sent between devices are 32-bit elements; how exact they have to be, the bound alone decides.
No kernel may reach another device: no remote copies, remote signals or barrier semaphores. Data moves between devices by JAX's collectives and lax.ppermute only.
A program may use at most 64 MiB of HBM per device.

```python
import jax
import jax.numpy as jnp
from jax import lax

LEAF = 512
RIGHT_SIDES = 64
EXPANSION_RANK = 64
LEAF_DEV = 4
NEAR_COUNT = 6
CELL_LIST = 4
BOX_LIST = 3
ITERS = 2
TOP_LIST = 4
LEAVES = 2048
POINTS = 1048576
CELLS = 512
GROUP = 32
BOXES = 16
COARSE_BOXES = 8


def row_orders(key, rows, count):

    def one_row(row_key):
        return jax.random.permutation(row_key, count)
    return jax.vmap(one_row)(jax.random.split(key, rows)).astype(jnp.int32)


def xor_pattern(key, constant, groups, members, count):
    key = jax.random.fold_in(key, constant)
    label_key, mask_key = jax.random.split(key)
    labels = row_orders(label_key, groups, members)
    masks = row_orders(mask_key, groups, members - 1)[:, :count] + 1
    return (labels, masks)


def fixed_pattern(members, count):
    labels = jnp.arange(members, dtype=jnp.int32)[None, :]
    masks = jnp.arange(1, count + 1, dtype=jnp.int32)[None, :]
    return (labels, masks)


def pattern_lists(labels, masks):
    groups = labels.shape[0]
    members = labels.shape[1]
    inverse = jnp.argsort(labels, axis=1).astype(jnp.int32)
    flipped = jnp.bitwise_xor(labels[:, :, None], masks[:, None, :])
    group_ids = jnp.arange(groups, dtype=jnp.int32)[:, None, None]
    partners = inverse[group_ids, flipped]
    return (group_ids * members + partners).reshape(groups * members, masks.shape[1]).astype(jnp.int32)


def paired_blocks(key, labels, masks, fan_in):
    groups = labels.shape[0]
    members = labels.shape[1]
    count = masks.shape[1]
    flipped = jnp.bitwise_xor(labels[:, :, None], masks[:, None, :])
    first = jnp.minimum(labels[:, :, None], flipped)
    raw = jax.random.normal(key, (groups, count, members, EXPANSION_RANK, EXPANSION_RANK), jnp.float32) * fan_in ** (-0.5)
    group_ids = jnp.arange(groups, dtype=jnp.int32)[:, None, None]
    slot_ids = jnp.arange(count, dtype=jnp.int32)[None, None, :]
    blocks = raw[group_ids, slot_ids, first]
    upper = labels[:, :, None] < flipped
    blocks = jnp.where(upper[:, :, :, None, None], blocks, jnp.swapaxes(blocks, -1, -2))
    return blocks.reshape(groups * members, count, EXPANSION_RANK, EXPANSION_RANK)


def draw_points(key, part):
    key = jax.random.fold_in(key, 11)
    leaf_index = jnp.arange(POINTS, dtype=jnp.int32) // LEAF
    coords = []
    for axis_bit in range(3):
        cell_coord = jnp.zeros((POINTS,), jnp.int32)
        for depth_bit in range(11):
            bit_value = jnp.bitwise_and(jnp.right_shift(leaf_index, 3 * depth_bit + axis_bit), 1)
            cell_coord = cell_coord + jnp.left_shift(bit_value, depth_bit)
        coords.append(cell_coord.astype(jnp.float32))
    corner = jnp.stack(coords)
    return corner + jax.random.uniform(key, (3, POINTS), jnp.float32)


def draw_neighbours(key, part):
    key = jax.random.fold_in(key, 12)
    block_count = LEAVES // 8
    others = jnp.array([1, 2, 3, 5, 6, 7], dtype=jnp.int32)
    orders = row_orders(key, block_count, 6)[:, :NEAR_COUNT - 2]
    masks = jnp.concatenate([jnp.zeros((block_count, 1), jnp.int32), jnp.full((block_count, 1), 4, jnp.int32), others[orders]], axis=1)
    leaf_ids = jnp.arange(LEAVES, dtype=jnp.int32)
    return jnp.bitwise_xor(leaf_ids[:, None], masks[leaf_ids // 8]).astype(jnp.int32)


def draw_cell_lists(key, part):
    labels, masks = xor_pattern(key, 21, CELLS // GROUP, GROUP, CELL_LIST)
    return pattern_lists(labels, masks)


def draw_cell_coupling(key, part):
    labels, masks = xor_pattern(key, 21, CELLS // GROUP, GROUP, CELL_LIST)
    key = jax.random.fold_in(key, 16)
    return paired_blocks(key, labels, masks, EXPANSION_RANK * CELL_LIST * LEAF_DEV)


def draw_box_coupling(key, part):
    key = jax.random.fold_in(key, 17)
    labels, masks = fixed_pattern(BOXES, BOX_LIST)
    return paired_blocks(key, labels, masks, EXPANSION_RANK * BOX_LIST * LEAF_DEV * GROUP)


def draw_top_coupling(key, part):
    key = jax.random.fold_in(key, 18)
    labels, masks = fixed_pattern(COARSE_BOXES, TOP_LIST)
    return paired_blocks(key, labels, masks, EXPANSION_RANK * TOP_LIST * LEAF_DEV * GROUP * 2)


def block_scale(key, shape, cuts, smallest, high):
    gain = 1.0
    for dim, shards_of in cuts:
        draws = jax.random.uniform(jax.random.fold_in(jax.random.fold_in(key, 6), dim), (shards_of,), jnp.float32, smallest / len(cuts), high / len(cuts))
        gain = gain * jnp.repeat(jnp.exp(draws), shape[dim] // shards_of).reshape((-1,) + (1,) * (len(shape) - 1 - dim))
    return gain


def centred(own_key, extent, spread, most, cuts=(), kind=jnp.bfloat16):
    values = spread * jax.random.normal(own_key, extent, jnp.float32)
    if cuts:
        values = values * block_scale(own_key, extent, cuts, -0.22, 0.18)
    return jnp.clip(values, -most, most).astype(kind)


def setup_inputs(seed: int = 0) -> dict:
    arg_keys = jax.random.split(jax.random.key(seed), 12)
    points = draw_points(jax.random.fold_in(arg_keys[11], 71), 0)
    targets = centred(arg_keys[1], (RIGHT_SIDES, POINTS), 1.0, 6.0, ((1, 512),), jnp.float32)
    basis = centred(arg_keys[2], (LEAVES, EXPANSION_RANK, LEAF), LEAF ** -0.5, 0.25, ((0, 512),), jnp.float32)
    leaf_transfer = centred(arg_keys[3], (LEAVES, EXPANSION_RANK, EXPANSION_RANK), EXPANSION_RANK ** -0.5, 0.75, ((0, 512),), jnp.float32)
    cell_transfer = centred(arg_keys[4], (CELLS, EXPANSION_RANK, EXPANSION_RANK), EXPANSION_RANK ** -0.5, 0.75, ((0, 512),), jnp.float32)
    box_parent_transfer = centred(arg_keys[5], (BOXES, EXPANSION_RANK, EXPANSION_RANK), EXPANSION_RANK ** -0.5, 0.75, (), jnp.float32)
    cell_coupling = draw_cell_coupling(jax.random.fold_in(arg_keys[11], 71), 0)
    box_coupling = draw_box_coupling(jax.random.fold_in(arg_keys[11], 71), 0)
    top_coupling = draw_top_coupling(jax.random.fold_in(arg_keys[11], 71), 0)
    neighbours = draw_neighbours(jax.random.fold_in(arg_keys[11], 71), 0)
    cell_lists = draw_cell_lists(jax.random.fold_in(arg_keys[11], 71), 0)
    return dict(points=points, targets=targets, basis=basis, leaf_transfer=leaf_transfer, cell_transfer=cell_transfer, box_parent_transfer=box_parent_transfer, cell_coupling=cell_coupling, box_coupling=box_coupling, top_coupling=top_coupling, neighbours=neighbours, cell_lists=cell_lists)


kernel_rate = 3.4641016151377544
near_weight = 0.0625
noise_level = 1.0
exact_solution = lax.Precision.HIGHEST

def matern(dist_sq):
    scaled = kernel_rate * jnp.sqrt(dist_sq)
    return (1.0 + scaled) * jnp.exp(-scaled)

def xor_lists(count, length):
    return jnp.bitwise_xor(jnp.arange(count, dtype=jnp.int32)[:, None], jnp.arange(1, length + 1, dtype=jnp.int32)[None, :]).astype(jnp.int32)

def near_apply(points, direction, neighbours):
    leaf_points = points.reshape(3, LEAVES, LEAF).transpose(1, 0, 2)
    vectors = direction.reshape(RIGHT_SIDES, LEAVES, LEAF)

    def one_leaf(leaf_item):
        own_points, near_rows = leaf_item
        near_points = jnp.take(leaf_points, near_rows, axis=0)
        chosen = jnp.take(vectors, near_rows, axis=1)
        dist_sq = jnp.zeros((near_rows.shape[0], LEAF, LEAF), jnp.float32)
        for coordinate in range(3):
            offset = near_points[:, coordinate, :, None] - own_points[None, coordinate, None, :]
            dist_sq = dist_sq + offset * offset
        tiles = matern(dist_sq)
        return jnp.einsum('cnj,nji->ci', chosen, tiles, precision=exact_solution)
    result = lax.map(one_leaf, (leaf_points, neighbours), batch_size=16)
    return near_weight * result.transpose(1, 0, 2).reshape(RIGHT_SIDES, POINTS)

def far_apply(direction, basis, leaf_transfer, cell_transfer, box_parent_transfer, cell_coupling, box_coupling, top_coupling, cell_lists):
    box_lists = xor_lists(BOXES, BOX_LIST)
    top_lists = xor_lists(COARSE_BOXES, TOP_LIST)
    vectors = direction.reshape(RIGHT_SIDES, LEAVES, LEAF)
    leaf_moments = jnp.einsum('akj,caj->akc', basis, vectors, precision=exact_solution)
    cell_moments = jnp.einsum('akl,akc->alc', leaf_transfer, leaf_moments, precision=exact_solution).reshape(CELLS, LEAF_DEV, EXPANSION_RANK, RIGHT_SIDES).sum(axis=1)
    box_moment_terms = jnp.einsum('bkl,bkc->blc', cell_transfer, cell_moments, precision=exact_solution).reshape(BOXES, GROUP, EXPANSION_RANK, RIGHT_SIDES).sum(axis=1)
    coarse_moments = jnp.einsum('qpf,qpj->qfj', box_parent_transfer, box_moment_terms, precision=exact_solution).reshape(COARSE_BOXES, 2, EXPANSION_RANK, RIGHT_SIDES).sum(axis=1)
    coarse_local = jnp.einsum('tskl,tslc->tkc', top_coupling, coarse_moments[top_lists], precision=exact_solution)
    box_local_terms = jnp.einsum('spt,sti->spi', box_parent_transfer, jnp.repeat(coarse_local, 2, axis=0), precision=exact_solution)
    box_local_terms = box_local_terms + jnp.einsum('gskl,gslc->gkc', box_coupling, box_moment_terms[box_lists], precision=exact_solution)
    cell_local = jnp.einsum('bkl,blc->bkc', cell_transfer, jnp.repeat(box_local_terms, GROUP, axis=0), precision=exact_solution)
    cell_local = cell_local + jnp.einsum('bskl,bslc->bkc', cell_coupling, cell_moments[cell_lists], precision=exact_solution)
    leaf_local = jnp.einsum('akl,alc->akc', leaf_transfer, jnp.repeat(cell_local, LEAF_DEV, axis=0), precision=exact_solution)
    return jnp.einsum('akj,akc->caj', basis, leaf_local, precision=exact_solution).reshape(RIGHT_SIDES, POINTS)

def reference(points, targets, basis, leaf_transfer, cell_transfer, box_parent_transfer, cell_coupling, box_coupling, top_coupling, neighbours, cell_lists):

    def apply_operator(direction):
        near = near_apply(points, direction, neighbours)
        far = far_apply(direction, basis, leaf_transfer, cell_transfer, box_parent_transfer, cell_coupling, box_coupling, top_coupling, cell_lists)
        return noise_level * direction + near + far
    solution = jnp.zeros_like(targets)
    residual = targets
    direction = targets
    norm_now = lax.optimization_barrier(jnp.sum(residual * residual, axis=1))
    for iteration in range(ITERS):
        image = apply_operator(direction)
        alpha = norm_now / lax.optimization_barrier(jnp.sum(direction * image, axis=1))
        solution = solution + alpha[:, None] * direction
        residual = residual - alpha[:, None] * image
        if iteration + 1 < ITERS:
            norm_next = lax.optimization_barrier(jnp.sum(residual * residual, axis=1))
            direction = residual + (norm_next / norm_now)[:, None] * direction
            norm_now = norm_next
    return (solution, residual)
```

```python
import functools
import math

import jax
import jax.numpy as jnp
from jax import lax
from jax.experimental import pallas as pl
from jax.experimental.pallas import tpu as pltpu
from jax.sharding import PartitionSpec as P

RANK = 64
ROWS = 64
LEAF = 512
OWN = 4
SLOTS = 6
FEATURES = 32
BOX_SPAN = 9
GROUP = 32
LIST = 4

UNIT = 2.0 * math.sqrt(3.0)
NEAR_WEIGHT = 0.0625

EXACT = lax.Precision.HIGHEST
VMEM = pl.BlockSpec(memory_space=pltpu.VMEM)
SMEM = pl.BlockSpec(memory_space=pltpu.SMEM)
ANY = pl.BlockSpec(memory_space=pl.ANY)

NN = (((1,), (0,)), ((), ()))
NT = (((1,), (1,)), ((), ()))
TN = (((0,), (0,)), ((), ()))


def mm(a, b, dims=NN):
    return lax.dot_general(a, b, dims, precision=EXACT, preferred_element_type=jnp.float32)


def mm16(a, b, dims=NN):
    return lax.dot_general(a, b, dims, preferred_element_type=jnp.float32)


def split2(value):
    high = value.astype(jnp.bfloat16)
    return high, (value - high.astype(jnp.float32)).astype(jnp.bfloat16)


def split3(value):
    first = value.astype(jnp.bfloat16).astype(jnp.float32)
    rest = value - first
    second = rest.astype(jnp.bfloat16).astype(jnp.float32)
    return first, second, rest - second


def params(mib=32):
    return pltpu.CompilerParams(vmem_limit_bytes=mib * 1024 * 1024)


def cost(flops, moved, special=0):
    return pl.CostEstimate(flops=flops, bytes_accessed=moved, transcendentals=special)


def shape(*dims, dtype=jnp.float32):
    return jax.ShapeDtypeStruct(dims, dtype)


def packed_rows(table):
    return jnp.concatenate([table[: ROWS // 2], table[ROWS // 2 :]], axis=1)


def unpacked_rows(table):
    return jnp.concatenate([table[:, :RANK], table[:, RANK:]], axis=0)


def fetch(pairs, sems):
    copies = [
        pltpu.make_async_copy(source, target, sems.at[k])
        for k, (source, target) in enumerate(pairs)
    ]
    for copy in copies:
        copy.start()
    return copies


def up_body(
    basis, leaf_transfer, cell_transfer, lists, vector, lifts, message, cell, b, t, c, v, sems
):
    copies = fetch(
        ((leaf_transfer, t), (basis, b), (vector, v), (cell_transfer, c)), sems
    )
    for copy in copies:
        copy.wait()
    total = jnp.zeros((ROWS, RANK), jnp.float32)
    for a in range(OWN):
        lift = mm(t[a], b[a], TN)
        lifts[:, a * LEAF : (a + 1) * LEAF] = lift
        total = total + mm(v[:, a * LEAF : (a + 1) * LEAF], lift, NT)
    message[:, 0, 0:128] = packed_rows(total)
    message[:, 0, 128:256] = packed_rows(mm(total, c[0]))
    lane = lax.broadcasted_iota(jnp.int32, (GROUP, 128), 1)
    table = jnp.zeros((GROUP, 128), jnp.int32)
    for k in range(LIST):
        table = jnp.where(lane == k, lists[0, k] & (GROUP - 1), table)
    message[:, 0, 256:384] = table.astype(jnp.float32)
    cell[:, :RANK] = c[0]
    cell[:, RANK:] = c[0]


def up(basis, leaf_transfer, cell_transfer, cell_lists, vector):
    return pl.pallas_call(
        up_body,
        out_shape=(
            shape(RANK, OWN * LEAF),
            shape(GROUP, 1, 384),
            shape(RANK, 2 * RANK),
        ),
        in_specs=[ANY] * 3 + [SMEM, ANY],
        out_specs=[VMEM] * 3,
        scratch_shapes=[
            pltpu.VMEM((OWN, RANK, LEAF), jnp.float32),
            pltpu.VMEM((OWN, RANK, RANK), jnp.float32),
            pltpu.VMEM((1, RANK, RANK), jnp.float32),
            pltpu.VMEM((ROWS, OWN * LEAF), jnp.float32),
            pltpu.SemaphoreType.DMA((4,)),
        ],
        compiler_params=params(60),
        cost_estimate=cost(60_000_000, 2_000_000),
        name="up",
    )(basis, leaf_transfer, cell_transfer, cell_lists, vector)


def coarse_body(parent_ref, box_ref, top_ref, out, parent, box_coupling, top_coupling, sems):
    g = lax.axis_index("gx")
    t = g // 2
    copies = fetch(
        (
            (parent_ref, parent),
            (box_ref.at[g], box_coupling),
            (top_ref.at[t], top_coupling),
        ),
        sems,
    )
    out[...] = jnp.zeros_like(out)
    for copy in copies:
        copy.wait()
    for m in range(1, BOX_SPAN + 1):
        if m >= 2:
            if m % 2 == 0:
                through = mm(parent[g], top_coupling[m // 2 - 1])
            value = mm(parent[jnp.bitwise_xor(g, m)], through, NT)
        if m <= 3:
            direct = box_coupling[m - 1].T
            value = direct if m == 1 else value + direct
        low = (m - 1) * 128
        out[low : low + 64, 0:64] = value
        out[low + 64 : low + 128, 64:128] = value


def coarse(parent, box_coupling, top_coupling):
    return pl.pallas_call(
        coarse_body,
        out_shape=shape(BOX_SPAN * 128, 128),
        in_specs=[ANY] * 3,
        out_specs=VMEM,
        scratch_shapes=[
            pltpu.VMEM((16, RANK, RANK), jnp.float32),
            pltpu.VMEM((3, RANK, RANK), jnp.float32),
            pltpu.VMEM((4, RANK, RANK), jnp.float32),
            pltpu.SemaphoreType.DMA((3,)),
        ],
        compiler_params=params(60),
        cost_estimate=cost(50_000_000, 2_000_000),
        name="coarse",
    )(parent, box_coupling, top_coupling)


def route_body(received, box, picked):
    chunk = jnp.sum(received[:, 0, 128:256], axis=0, keepdims=True)
    box[...] = jnp.broadcast_to(chunk[None], box.shape)
    cells = received[:, 0, 0:128]
    numbers = received[:, 0, 256:384]
    member = lax.broadcasted_iota(jnp.int32, (GROUP, GROUP), 1).astype(jnp.float32)
    for k in range(LIST):
        chooser = (numbers[:, k : k + 1] == member).astype(jnp.float32)
        picked[:, k * 128 : (k + 1) * 128] = mm(chooser, cells)


def route(received):
    return pl.pallas_call(
        route_body,
        out_shape=(shape(16, 1, 128), shape(GROUP, LIST * 128)),
        in_specs=[VMEM],
        out_specs=[VMEM] * 2,
        compiler_params=params(),
        cost_estimate=cost(4_000_000, 200_000),
        name="route",
    )(received)


def boxes_body(received, maps, picked, message):
    g = lax.axis_index("gx")
    row = jnp.concatenate(
        [received[jnp.bitwise_xor(g, m)] for m in range(1, BOX_SPAN + 1)], axis=1
    )
    local = mm(row, maps[...])
    message[:, 0, 0:128] = jnp.broadcast_to(local, (GROUP, 128))
    message[:, 0, 128:640] = picked[...]


def boxes(received, maps, picked):
    return pl.pallas_call(
        boxes_body,
        out_shape=shape(GROUP, 1, 640),
        in_specs=[VMEM] * 3,
        out_specs=VMEM,
        compiler_params=params(),
        cost_estimate=cost(4_000_000, 200_000),
        name="boxes",
    )(received, maps, picked)


def sum_rows(columns):
    lane = lax.broadcasted_iota(jnp.int32, (ROWS, 128), 1)
    table = jnp.zeros((ROWS, 128), jnp.float32)
    for k, column in columns:
        table = jnp.where(lane == k, column, table)
    table = table.T
    upper = jnp.concatenate([table[0:1], table[1:2]], axis=1)
    lower = jnp.concatenate([table[2:3], table[3:4]], axis=1)
    return jnp.concatenate([upper, lower], axis=0)


def tally_body(
    lists, received, cells, couplings, moment, dots, image, near, box, local, sums
):
    total = mm(received[...], cells[:, :RANK], TN)
    box[...] = jnp.broadcast_to(packed_rows(total)[None], box.shape)
    expansion = jnp.zeros((RANK, ROWS), jnp.float32)
    for k in range(LIST):
        low = pl.multiple_of((lists[0, k] & (GROUP - 1)) * RANK, RANK)
        expansion = expansion + mm(couplings[0, k], received[pl.ds(low, RANK), :])
    local[...] = expansion
    square = dots[:, 2:3]
    cubic = square
    for a in range(OWN):
        part = slice(a * LEAF, (a + 1) * LEAF)
        cubic = cubic + jnp.sum(image[:, part] * near[:, part], axis=1, keepdims=True)
    rows = sum_rows(((0, dots[:, 0:1]), (1, dots[:, 1:2]), (2, square), (3, cubic)))
    far = jnp.sum(moment[...] * expansion, axis=0, keepdims=True)
    blank = jnp.zeros((1, RANK), jnp.float32)
    rows = rows + jnp.concatenate(
        [jnp.zeros((1, 128), jnp.float32), jnp.concatenate([blank, far], axis=1)], axis=0
    )
    sums[...] = jnp.broadcast_to(rows[None], sums.shape)


def tally(lists, received, cells, couplings, moment, dots, image, near):
    return pl.pallas_call(
        tally_body,
        out_shape=(shape(16, 32, 128), shape(RANK, ROWS), shape(GROUP, 2, 128)),
        in_specs=[SMEM] + [VMEM] * 7,
        out_specs=[VMEM] * 3,
        compiler_params=params(),
        cost_estimate=cost(4_000_000, 2_500_000),
        name="tally",
    )(lists, received, cells, couplings, moment, dots, image, near)


def spread_body(received, extra, sums):
    total = jnp.sum(received[...], axis=0, keepdims=True) + extra[...][None]
    sums[...] = jnp.broadcast_to(total, sums.shape)


def spread(received, extra):
    return pl.pallas_call(
        spread_body,
        out_shape=shape(16, 2, 128),
        in_specs=[VMEM] * 2,
        out_specs=VMEM,
        compiler_params=params(),
        cost_estimate=cost(10_000, 50_000),
        name="spread",
    )(received, extra)


def features_body(own, partner, left, right, rows):
    block = lax.axis_index("gx") * (lax.axis_size("gy") // 2) + lax.axis_index("gy") // 2
    axis_id = lax.broadcasted_iota(jnp.int32, (3, OWN * LEAF), 0)
    centre = jnp.zeros((3, OWN * LEAF), jnp.int32)
    for axis in range(3):
        place = 1
        for depth in range(1, 11):
            place = place + ((block >> (3 * (depth - 1) + axis)) & 1) * (1 << depth)
        centre = jnp.where(axis_id == axis, place, centre)
    centre = centre.astype(jnp.float32)
    ones = jnp.ones((3, OWN * LEAF), jnp.float32)
    for half, source in enumerate((own, partner)):
        local = (source[...] - centre) * UNIT
        one, two, three = split3(local)
        square = jnp.sum(local * local, axis=0, keepdims=True)
        squares = split3(square)
        rows[24:32, :] = jnp.zeros((8, OWN * LEAF), jnp.float32)
        for place, piece in enumerate((one, one, two, one, two, three)):
            rows[3 * place : 3 * place + 3, :] = -2.0 * piece
        for place, piece in enumerate(squares):
            rows[18 + place : 19 + place, :] = piece
        rows[21:24, :] = ones
        for a in range(OWN):
            left[half * OWN + a] = rows[:, a * LEAF : (a + 1) * LEAF].T.astype(jnp.bfloat16)
        if half == 0:
            for place, piece in enumerate((one, two, one, three, two, one)):
                rows[3 * place : 3 * place + 3, :] = piece
            rows[18:21, :] = ones
            for place, piece in enumerate(squares):
                rows[21 + place : 22 + place, :] = piece
            for a in range(OWN):
                right[a] = rows[:, a * LEAF : (a + 1) * LEAF].astype(jnp.bfloat16)


def features(own, partner):
    return pl.pallas_call(
        features_body,
        out_shape=(
            shape(2 * OWN, LEAF, FEATURES, dtype=jnp.bfloat16),
            shape(OWN, FEATURES, LEAF, dtype=jnp.bfloat16),
        ),
        in_specs=[VMEM] * 2,
        out_specs=[VMEM] * 2,
        scratch_shapes=[pltpu.VMEM((FEATURES, OWN * LEAF), jnp.float32)],
        compiler_params=params(),
        cost_estimate=cost(1_000_000, 400_000),
        name="features",
    )(own, partner)


def joined_body(own, partner, out):
    for half, source in enumerate((own, partner)):
        for a in range(OWN):
            high, low = split2(source[:, a * LEAF : (a + 1) * LEAF])
            out[half * OWN + a, :ROWS, :] = high
            out[half * OWN + a, ROWS:, :] = low


def joined(own, partner):
    return pl.pallas_call(
        joined_body,
        out_shape=shape(2 * OWN, 2 * ROWS, LEAF, dtype=jnp.bfloat16),
        in_specs=[VMEM] * 2,
        out_specs=VMEM,
        compiler_params=params(),
        cost_estimate=cost(1_000_000, 2_000_000),
        name="joined",
    )(own, partner)


def neighbour_row(neighbours, leaf, n):
    parity = lax.axis_index("gy") % 2
    return jnp.bitwise_xor(neighbours[leaf, n] & (2 * OWN - 1), OWN * parity)


def tiles_body(neighbours, left, right, vectors, tiles, out, square):
    leaf = pl.program_id(0)
    target = right[leaf]
    rows = [neighbour_row(neighbours, leaf, n) for n in range(SLOTS)]
    wide = jnp.zeros((2 * ROWS, LEAF), jnp.float32)
    narrow = jnp.zeros((ROWS, LEAF), jnp.float32)
    step = 32

    def measure(n):
        square[n % 2] = mm16(left[rows[n]], target)

    def apply(n, wide, narrow):
        wide = wide + mm16(vectors[rows[n]], tiles[0, n, 0])
        narrow = narrow + mm16(vectors[rows[n], :ROWS, :], tiles[0, n, 1])
        return wide, narrow

    measure(0)
    for n in range(SLOTS):
        if n + 1 < SLOTS:
            measure(n + 1)
        if n > 0:
            wide, narrow = apply(n - 1, wide, narrow)
        for low in range(0, LEAF, step):
            part = jnp.maximum(square[n % 2, low : low + step, :], 1e-12)
            u = part * lax.rsqrt(part)
            kernel = jnp.exp(-u) * (1.0 + u)
            high, rest = split2(kernel)
            tiles[0, n, 0, low : low + step, :] = high
            tiles[0, n, 1, low : low + step, :] = rest
    wide, narrow = apply(SLOTS - 1, wide, narrow)
    out[...] = NEAR_WEIGHT * (wide[:ROWS] + wide[ROWS:] + narrow)


def near_tiles(neighbours, left, right, vectors):
    tile = shape(OWN, SLOTS, 2, LEAF, LEAF, dtype=jnp.bfloat16)
    block = pl.BlockSpec((1, SLOTS, 2, LEAF, LEAF), lambda a: (a, 0, 0, 0, 0))
    return pl.pallas_call(
        tiles_body,
        grid=(OWN,),
        out_shape=(tile, shape(ROWS, OWN * LEAF)),
        in_specs=[SMEM] + [VMEM] * 3,
        out_specs=[block, pl.BlockSpec((ROWS, LEAF), lambda a: (0, a))],
        scratch_shapes=[pltpu.VMEM((2, LEAF, LEAF), jnp.float32)],
        compiler_params=params(40),
        cost_estimate=cost(8_000_000_000, 30_000_000, 12_000_000),
        name="near_tiles",
    )(neighbours, left, right, vectors)


def again_body(neighbours, vectors, high_tiles, low_tiles, out):
    leaf = pl.program_id(0)
    wide = jnp.zeros((2 * ROWS, LEAF), jnp.float32)
    narrow = jnp.zeros((ROWS, LEAF), jnp.float32)
    for n in range(SLOTS // 2):
        row = neighbour_row(neighbours, leaf, pl.program_id(1) * (SLOTS // 2) + n)
        wide = wide + mm16(vectors[row], high_tiles[0, n, 0])
        narrow = narrow + mm16(vectors[row, :ROWS, :], low_tiles[0, n, 0])
    value = NEAR_WEIGHT * (wide[:ROWS] + wide[ROWS:] + narrow)

    @pl.when(pl.program_id(1) == 0)
    def first():
        out[...] = value

    @pl.when(pl.program_id(1) > 0)
    def later():
        out[...] += value


def near_again(neighbours, vectors, tiles):
    half = (1, SLOTS // 2, 1, LEAF, LEAF)
    high = pl.BlockSpec(half, lambda a, h: (a, h, 0, 0, 0))
    low = pl.BlockSpec(half, lambda a, h: (a, h, 1, 0, 0))
    return pl.pallas_call(
        again_body,
        grid=(OWN, 2),
        out_shape=shape(ROWS, OWN * LEAF),
        in_specs=[SMEM, VMEM, high, low],
        out_specs=pl.BlockSpec((ROWS, LEAF), lambda a, h: (0, a)),
        compiler_params=params(40),
        cost_estimate=cost(6_000_000_000, 30_000_000),
        name="near_again",
    )(neighbours, vectors, tiles, tiles)


def box_local(maps, boxes):
    g = lax.axis_index("gx")
    row = jnp.concatenate(
        [boxes[jnp.bitwise_xor(g, m)] for m in range(1, BOX_SPAN + 1)], axis=1
    )
    return mm(row, maps[...])


def cell_local(couplings, cell_transfer, received):
    local = mm(unpacked_rows(received[:, 0, 0:128]), cell_transfer[0], NT)
    for s in range(LIST):
        low = 128 * (s + 1)
        local = local + mm(
            unpacked_rows(received[:, 0, low : low + 128]), couplings[0, s], NT
        )
    return local


def middle_body(
    couplings, cell_transfer, lifts, vector, near, received, image, moment, dots
):
    local = cell_local(couplings, cell_transfer, received)
    total = jnp.zeros((RANK, ROWS), jnp.float32)
    sums = [jnp.zeros((ROWS, 1), jnp.float32)] * 3
    for a in range(OWN):
        part = slice(a * LEAF, (a + 1) * LEAF)
        lift = lifts[:, part]
        value = vector[:, part]
        result = value + near[:, part] + mm(local, lift)
        image[:, part] = result
        total = total + mm(lift, result, NT)
        for k, product in enumerate((value * value, value * result, result * result)):
            sums[k] = sums[k] + jnp.sum(product, axis=1, keepdims=True)
    moment[...] = total
    lane = lax.broadcasted_iota(jnp.int32, (ROWS, 128), 1)
    table = jnp.zeros((ROWS, 128), jnp.float32)
    for k, column in enumerate(sums):
        table = jnp.where(lane == k, column, table)
    dots[...] = table


def middle(couplings, cell_transfer, lifts, vector, near, received):
    return pl.pallas_call(
        middle_body,
        out_shape=(shape(ROWS, OWN * LEAF), shape(RANK, ROWS), shape(ROWS, 128)),
        in_specs=[VMEM] * 6,
        out_specs=[VMEM] * 3,
        compiler_params=params(),
        cost_estimate=cost(80_000_000, 3_000_000),
        name="middle",
    )(couplings, cell_transfer, lifts, vector, near, received)


def last_body(cell_transfer, maps, local, lifts, vector, near, boxes, image, extra):
    row = box_local(maps, boxes)
    product = unpacked_rows(row * boxes[lax.axis_index("gx")])
    extra[...] = sum_rows(((3, jnp.sum(product, axis=1, keepdims=True)),))
    expansion = local[...] + mm(cell_transfer[0], unpacked_rows(row), NT)
    for a in range(OWN):
        part = slice(a * LEAF, (a + 1) * LEAF)
        image[:, part] = vector[:, part] + near[:, part] + mm(expansion, lifts[:, part], TN)


def last(cell_transfer, maps, local, lifts, vector, near, boxes):
    return pl.pallas_call(
        last_body,
        out_shape=(shape(ROWS, OWN * LEAF), shape(2, 128)),
        in_specs=[VMEM] * 7,
        out_specs=[VMEM] * 2,
        compiler_params=params(),
        cost_estimate=cost(40_000_000, 3_000_000),
        name="last",
    )(cell_transfer, maps, local, lifts, vector, near, boxes)


def finish_body(received, vector, first, second, iterate, residual):
    table = jnp.sum(received[...], axis=0)
    table = jnp.concatenate([table, jnp.zeros((6, 128), jnp.float32)], axis=0).T
    norm = table[:ROWS, 0:1]
    lean = table[ROWS:, 0:1]
    square = table[:ROWS, 1:2]
    cubic = table[ROWS:, 1:2]
    alpha0 = norm / lean
    norm1 = alpha0 * (alpha0 * square - lean)
    beta = norm1 / norm
    grow = 1.0 + beta
    curve = grow * (grow * lean - 2.0 * alpha0 * square) + alpha0 * alpha0 * cubic
    alpha1 = norm1 / curve
    iterate[...] = (alpha0 + alpha1 * grow) * vector[...] - (alpha1 * alpha0) * first[...]
    residual[...] = (
        vector[...]
        - (alpha0 + alpha1 * grow) * first[...]
        + (alpha1 * alpha0) * second[...]
    )


def finish(received, vector, first, second):
    return pl.pallas_call(
        finish_body,
        out_shape=(shape(ROWS, OWN * LEAF), shape(ROWS, OWN * LEAF)),
        in_specs=[VMEM] * 4,
        out_specs=[VMEM] * 2,
        compiler_params=params(),
        cost_estimate=cost(1_000_000, 3_000_000),
        name="finish",
    )(received, vector, first, second)


def exchange(block, axis, mask):
    count = lax.axis_size(axis)
    return lax.ppermute(block, axis, [(i, i ^ mask) for i in range(count)])


def turn(block, axis):
    return lax.all_to_all(block, axis, 0, 0, tiled=True)


def gathered(block):
    return lax.all_gather(block, "gy", axis=0, tiled=True)


def shards(
    points,
    targets,
    basis,
    leaf_transfer,
    cell_transfer,
    box_parent_transfer,
    cell_coupling,
    box_coupling,
    top_coupling,
    neighbours,
    cell_lists,
):
    partner_points = exchange(points, "gy", 1)
    partner_targets = exchange(targets, "gy", 1)
    lifts, message, cell = up(basis, leaf_transfer, cell_transfer, cell_lists, targets)
    cells = gathered(cell)
    maps = coarse(box_parent_transfer, box_coupling, top_coupling)
    left, right = features(points, partner_points)
    vectors = joined(targets, partner_targets)
    tiles, near = near_tiles(neighbours, left, right, vectors)
    box, picked = route(turn(message, "gy"))
    message = boxes(turn(box, "gx"), maps, picked)
    first, moment, dots = middle(
        cell_coupling, cell_transfer, lifts, targets, near, turn(message, "gy")
    )

    partner_first = exchange(first, "gy", 1)
    received = gathered(moment)
    near = near_again(neighbours, joined(first, partner_first), tiles)
    box, local, sums = tally(
        cell_lists, received, cells, cell_coupling, moment, dots, first, near
    )
    sums = turn(sums, "gy")
    second, extra = last(cell_transfer, maps, local, lifts, first, near, turn(box, "gx"))
    return finish(turn(spread(sums, extra), "gx"), targets, first, second)


def solution(mesh):
    both = ("gx", "gy")
    return jax.shard_map(
        shards,
        mesh=mesh,
        in_specs=(
            P(None, both),
            P(None, both),
            P(both, None, None),
            P(both, None, None),
            P(both, None, None),
            P(),
            P(both, None, None, None),
            P(),
            P(),
            P(both, None),
            P(both, None),
        ),
        out_specs=(P(None, both), P(None, both)),
        check_vma=False,
    )
```

```python
import functools
import math

import jax
import jax.numpy as jnp
from jax import lax
from jax.experimental import pallas as pl
from jax.experimental.pallas import tpu as pltpu
from jax.sharding import PartitionSpec as P

RANK = 64
ROWS = 64
LEAF = 512
OWN = 4
SLOTS = 6
FEATURES = 32
BOX_SPAN = 9
GROUP = 32
LIST = 4

UNIT = 2.0 * math.sqrt(3.0)
NEAR_WEIGHT = 0.0625

EXACT = lax.Precision.HIGHEST
VMEM = pl.BlockSpec(memory_space=pltpu.VMEM)
SMEM = pl.BlockSpec(memory_space=pltpu.SMEM)
ANY = pl.BlockSpec(memory_space=pl.ANY)

NN = (((1,), (0,)), ((), ()))
NT = (((1,), (1,)), ((), ()))
TN = (((0,), (0,)), ((), ()))


def mm(a, b, dims=NN):
    return lax.dot_general(a, b, dims, precision=EXACT, preferred_element_type=jnp.float32)


def mm16(a, b, dims=NN):
    return lax.dot_general(a, b, dims, preferred_element_type=jnp.float32)


def split2(value):
    high = value.astype(jnp.bfloat16)
    return high, (value - high.astype(jnp.float32)).astype(jnp.bfloat16)


def split3(value):
    first = value.astype(jnp.bfloat16).astype(jnp.float32)
    rest = value - first
    second = rest.astype(jnp.bfloat16).astype(jnp.float32)
    return first, second, rest - second


def params(mib=32):
    return pltpu.CompilerParams(vmem_limit_bytes=mib * 1024 * 1024)


def cost(flops, moved, special=0):
    return pl.CostEstimate(flops=flops, bytes_accessed=moved, transcendentals=special)


def shape(*dims, dtype=jnp.float32):
    return jax.ShapeDtypeStruct(dims, dtype)


def packed_rows(table):
    return jnp.concatenate([table[: ROWS // 2], table[ROWS // 2 :]], axis=1)


def unpacked_rows(table):
    return jnp.concatenate([table[:, :RANK], table[:, RANK:]], axis=0)


def fetch(pairs, sems):
    copies = [
        pltpu.make_async_copy(source, target, sems.at[k])
        for k, (source, target) in enumerate(pairs)
    ]
    for copy in copies:
        copy.start()
    return copies


def send_moments(message, moment, cell_transfer):
    message[:, 0, 0:128] = packed_rows(moment)
    message[:, 0, 128:256] = packed_rows(mm(moment, cell_transfer))


def up_body(
    basis, leaf_transfer, cell_transfer, lists, vector, points, lifts, message, v, p, b, t, c, sems
):
    copies = fetch(
        (
            (leaf_transfer, t),
            (basis, b),
            (vector, v),
            (cell_transfer, c),
            (points, p),
        ),
        sems,
    )
    for copy in copies:
        copy.wait()
    total = jnp.zeros((ROWS, RANK), jnp.float32)
    for a in range(OWN):
        lift = mm(t[a], b[a], TN)
        lifts[:, a * LEAF : (a + 1) * LEAF] = lift
        total = total + mm(v[:, a * LEAF : (a + 1) * LEAF], lift, NT)
    send_moments(message, total, c[0])
    lane = lax.broadcasted_iota(jnp.int32, (GROUP, 128), 1)
    table = jnp.zeros((GROUP, 128), jnp.int32)
    for k in range(LIST):
        table = jnp.where(lane == k, lists[0, k] & (GROUP - 1), table)
    message[:, 0, 256:384] = table.astype(jnp.float32)


def up(basis, leaf_transfer, cell_transfer, cell_lists, vector, points):
    return pl.pallas_call(
        up_body,
        out_shape=(
            shape(RANK, OWN * LEAF),
            shape(GROUP, 1, 384),
            shape(ROWS, OWN * LEAF),
            shape(3, OWN * LEAF),
        ),
        in_specs=[ANY] * 3 + [SMEM, ANY, ANY],
        out_specs=[VMEM] * 4,
        scratch_shapes=[
            pltpu.VMEM((OWN, RANK, LEAF), jnp.float32),
            pltpu.VMEM((OWN, RANK, RANK), jnp.float32),
            pltpu.VMEM((1, RANK, RANK), jnp.float32),
            pltpu.SemaphoreType.DMA((5,)),
        ],
        compiler_params=params(60),
        cost_estimate=cost(60_000_000, 2_000_000),
        name="up",
    )(basis, leaf_transfer, cell_transfer, cell_lists, vector, points)


def coarse_body(parent_ref, box_ref, top_ref, out, parent, box_coupling, top_coupling, sems):
    g = lax.axis_index("gx")
    t = g // 2
    copies = fetch(
        (
            (parent_ref, parent),
            (box_ref.at[g], box_coupling),
            (top_ref.at[t], top_coupling),
        ),
        sems,
    )
    out[...] = jnp.zeros_like(out)
    for copy in copies:
        copy.wait()
    for m in range(1, BOX_SPAN + 1):
        if m >= 2:
            if m % 2 == 0:
                through = mm(parent[g], top_coupling[m // 2 - 1])
            value = mm(parent[jnp.bitwise_xor(g, m)], through, NT)
        if m <= 3:
            direct = box_coupling[m - 1].T
            value = direct if m == 1 else value + direct
        low = (m - 1) * 128
        out[low : low + 64, 0:64] = value
        out[low + 64 : low + 128, 64:128] = value


def coarse(parent, box_coupling, top_coupling):
    return pl.pallas_call(
        coarse_body,
        out_shape=shape(BOX_SPAN * 128, 128),
        in_specs=[ANY] * 3,
        out_specs=VMEM,
        scratch_shapes=[
            pltpu.VMEM((16, RANK, RANK), jnp.float32),
            pltpu.VMEM((3, RANK, RANK), jnp.float32),
            pltpu.VMEM((4, RANK, RANK), jnp.float32),
            pltpu.SemaphoreType.DMA((3,)),
        ],
        compiler_params=params(60),
        cost_estimate=cost(50_000_000, 2_000_000),
        name="coarse",
    )(parent, box_coupling, top_coupling)


def route_body(with_lists, received, lists, *outs):
    box, picked = outs[0], outs[1]
    chunk = jnp.sum(received[:, 0, 128:256], axis=0, keepdims=True)
    box[...] = jnp.broadcast_to(chunk[None], box.shape)
    cells = received[:, 0, 0:128]
    numbers = received[:, 0, 256:384] if with_lists else lists[...]
    member = lax.broadcasted_iota(jnp.int32, (GROUP, GROUP), 1).astype(jnp.float32)
    for s in range(LIST):
        chooser = (numbers[:, s : s + 1] == member).astype(jnp.float32)
        picked[:, 0, s * 128 : (s + 1) * 128] = mm(chooser, cells)
    if with_lists:
        outs[2][...] = numbers


def route(received, lists=None):
    first = lists is None
    outs = (shape(16, 1, 128), shape(GROUP, 1, LIST * 128))
    if first:
        body = lambda received, *outs: route_body(True, received, None, *outs)
        outs = outs + (shape(GROUP, 128),)
        operands = (received,)
    else:
        body = functools.partial(route_body, False)
        operands = (received, lists)
    return pl.pallas_call(
        body,
        out_shape=outs,
        in_specs=[VMEM] * len(operands),
        out_specs=[VMEM] * len(outs),
        compiler_params=params(),
        cost_estimate=cost(4_000_000, 200_000),
        name="route",
    )(*operands)


def boxes_body(received, maps, picked, message):
    g = lax.axis_index("gx")
    row = jnp.concatenate(
        [received[jnp.bitwise_xor(g, m)] for m in range(1, BOX_SPAN + 1)], axis=1
    )
    local = mm(row, maps[...])
    message[:, 0, 0:128] = jnp.broadcast_to(local, (GROUP, 128))
    message[:, 0, 128:640] = picked[:, 0, :]


def boxes(received, maps, picked):
    return pl.pallas_call(
        boxes_body,
        out_shape=shape(GROUP, 1, 640),
        in_specs=[VMEM] * 3,
        out_specs=VMEM,
        compiler_params=params(),
        cost_estimate=cost(4_000_000, 200_000),
        name="boxes",
    )(received, maps, picked)


def sum_rows(columns):
    lane = lax.broadcasted_iota(jnp.int32, (ROWS, 128), 1)
    table = jnp.zeros((ROWS, 128), jnp.float32)
    for k, column in columns:
        table = jnp.where(lane == k, column, table)
    table = table.T
    upper = jnp.concatenate([table[0:1], table[1:2]], axis=1)
    lower = jnp.concatenate([table[2:3], table[3:4]], axis=1)
    return jnp.concatenate([upper, lower], axis=0)


def tally_body(
    couplings, maps, moment, dots, image, near, picked, received, local, chunk, sums
):
    expansion = jnp.zeros((ROWS, RANK), jnp.float32)
    for k in range(LIST):
        part = unpacked_rows(picked[:, 0, k * 128 : (k + 1) * 128])
        expansion = expansion + mm(part, couplings[0, k], NT)
    local[...] = expansion
    square = dots[:, 2:3]
    cubic = square + jnp.sum(moment[...] * expansion, axis=1, keepdims=True)
    for a in range(OWN):
        part = slice(a * LEAF, (a + 1) * LEAF)
        cubic = cubic + jnp.sum(image[:, part] * near[:, part], axis=1, keepdims=True)
    rows = sum_rows(((0, dots[:, 0:1]), (1, dots[:, 1:2]), (2, square), (3, cubic)))
    row = box_local(maps, received)
    chunk[...] = row
    product = row * received[lax.axis_index("gx")]
    place = lax.broadcasted_iota(jnp.int32, (2, 128), 0) * 128
    place = place + lax.broadcasted_iota(jnp.int32, (2, 128), 1)
    column = 128 + RANK + lax.axis_index("gy")
    for half in range(2):
        term = jnp.sum(product[:, half * RANK : (half + 1) * RANK], axis=1, keepdims=True)
        rows = rows + jnp.where(place == column + half * (ROWS // 2), term, 0.0)
    sums[...] = jnp.broadcast_to(rows[None], sums.shape)


def tally(couplings, maps, moment, dots, image, near, picked, received):
    return pl.pallas_call(
        tally_body,
        out_shape=(shape(ROWS, RANK), shape(1, 128), shape(16, 2, 128)),
        in_specs=[VMEM] * 8,
        out_specs=[VMEM] * 3,
        compiler_params=params(),
        cost_estimate=cost(4_000_000, 2_500_000),
        name="tally",
    )(couplings, maps, moment, dots, image, near, picked, received)


def spread_body(received, chunk, message):
    total = jnp.sum(received[...], axis=0)
    message[:, 0, 0:128] = jnp.broadcast_to(total[0:1], (GROUP, 128))
    message[:, 0, 128:256] = jnp.broadcast_to(total[1:2], (GROUP, 128))
    message[:, 0, 256:384] = jnp.broadcast_to(chunk[...], (GROUP, 128))


def spread(received, chunk):
    return pl.pallas_call(
        spread_body,
        out_shape=shape(GROUP, 1, 384),
        in_specs=[VMEM] * 2,
        out_specs=VMEM,
        compiler_params=params(),
        cost_estimate=cost(10_000, 50_000),
        name="spread",
    )(received, chunk)


def features_body(own, partner, left, right, rows):
    block = lax.axis_index("gx") * (lax.axis_size("gy") // 2) + lax.axis_index("gy") // 2
    axis_id = lax.broadcasted_iota(jnp.int32, (3, OWN * LEAF), 0)
    centre = jnp.zeros((3, OWN * LEAF), jnp.int32)
    for axis in range(3):
        place = 1
        for depth in range(1, 11):
            place = place + ((block >> (3 * (depth - 1) + axis)) & 1) * (1 << depth)
        centre = jnp.where(axis_id == axis, place, centre)
    centre = centre.astype(jnp.float32)
    ones = jnp.ones((3, OWN * LEAF), jnp.float32)
    for half, source in enumerate((own, partner)):
        local = (source[...] - centre) * UNIT
        one, two, three = split3(local)
        square = jnp.sum(local * local, axis=0, keepdims=True)
        squares = split3(square)
        rows[24:32, :] = jnp.zeros((8, OWN * LEAF), jnp.float32)
        for place, piece in enumerate((one, one, two, one, two, three)):
            rows[3 * place : 3 * place + 3, :] = -2.0 * piece
        for place, piece in enumerate(squares):
            rows[18 + place : 19 + place, :] = piece
        rows[21:24, :] = ones
        for a in range(OWN):
            left[half * OWN + a] = rows[:, a * LEAF : (a + 1) * LEAF].T.astype(jnp.bfloat16)
        if half == 0:
            for place, piece in enumerate((one, two, one, three, two, one)):
                rows[3 * place : 3 * place + 3, :] = piece
            rows[18:21, :] = ones
            for place, piece in enumerate(squares):
                rows[21 + place : 22 + place, :] = piece
            for a in range(OWN):
                right[a] = rows[:, a * LEAF : (a + 1) * LEAF].astype(jnp.bfloat16)


def features(own, partner):
    return pl.pallas_call(
        features_body,
        out_shape=(
            shape(2 * OWN, LEAF, FEATURES, dtype=jnp.bfloat16),
            shape(OWN, FEATURES, LEAF, dtype=jnp.bfloat16),
        ),
        in_specs=[VMEM] * 2,
        out_specs=[VMEM] * 2,
        scratch_shapes=[pltpu.VMEM((FEATURES, OWN * LEAF), jnp.float32)],
        compiler_params=params(),
        cost_estimate=cost(1_000_000, 400_000),
        name="features",
    )(own, partner)


def joined_body(own, partner, out):
    for half, source in enumerate((own, partner)):
        for a in range(OWN):
            high, low = split2(source[:, a * LEAF : (a + 1) * LEAF])
            out[half * OWN + a, :ROWS, :] = high
            out[half * OWN + a, ROWS:, :] = low


def joined(own, partner):
    return pl.pallas_call(
        joined_body,
        out_shape=shape(2 * OWN, 2 * ROWS, LEAF, dtype=jnp.bfloat16),
        in_specs=[VMEM] * 2,
        out_specs=VMEM,
        compiler_params=params(),
        cost_estimate=cost(1_000_000, 2_000_000),
        name="joined",
    )(own, partner)


def neighbour_row(neighbours, leaf, n):
    parity = lax.axis_index("gy") % 2
    return jnp.bitwise_xor(neighbours[leaf, n] & (2 * OWN - 1), OWN * parity)


def tiles_body(neighbours, left, right, vectors, tiles, out, square):
    leaf = pl.program_id(0)
    target = right[leaf]
    rows = [neighbour_row(neighbours, leaf, n) for n in range(SLOTS)]
    wide = jnp.zeros((2 * ROWS, LEAF), jnp.float32)
    narrow = jnp.zeros((ROWS, LEAF), jnp.float32)
    step = 32

    def measure(n):
        square[n % 2] = mm16(left[rows[n]], target)

    def apply(n, wide, narrow):
        wide = wide + mm16(vectors[rows[n]], tiles[0, n, 0])
        narrow = narrow + mm16(vectors[rows[n], :ROWS, :], tiles[0, n, 1])
        return wide, narrow

    measure(0)
    for n in range(SLOTS):
        if n + 1 < SLOTS:
            measure(n + 1)
        if n > 0:
            wide, narrow = apply(n - 1, wide, narrow)
        for low in range(0, LEAF, step):
            part = jnp.maximum(square[n % 2, low : low + step, :], 1e-12)
            u = part * lax.rsqrt(part)
            kernel = jnp.exp(-u) * (1.0 + u)
            high, rest = split2(kernel)
            tiles[0, n, 0, low : low + step, :] = high
            tiles[0, n, 1, low : low + step, :] = rest
    wide, narrow = apply(SLOTS - 1, wide, narrow)
    out[...] = NEAR_WEIGHT * (wide[:ROWS] + wide[ROWS:] + narrow)


def near_tiles(neighbours, left, right, vectors):
    tile = shape(OWN, SLOTS, 2, LEAF, LEAF, dtype=jnp.bfloat16)
    block = pl.BlockSpec((1, SLOTS, 2, LEAF, LEAF), lambda a: (a, 0, 0, 0, 0))
    return pl.pallas_call(
        tiles_body,
        grid=(OWN,),
        out_shape=(tile, shape(ROWS, OWN * LEAF)),
        in_specs=[SMEM] + [VMEM] * 3,
        out_specs=[block, pl.BlockSpec((ROWS, LEAF), lambda a: (0, a))],
        scratch_shapes=[pltpu.VMEM((2, LEAF, LEAF), jnp.float32)],
        compiler_params=params(40),
        cost_estimate=cost(8_000_000_000, 30_000_000, 12_000_000),
        name="near_tiles",
    )(neighbours, left, right, vectors)


def again_body(neighbours, vectors, high_tiles, low_tiles, box, out, box_out):
    box_out[...] = box[...]
    leaf = pl.program_id(0)
    wide = jnp.zeros((2 * ROWS, LEAF), jnp.float32)
    narrow = jnp.zeros((ROWS, LEAF), jnp.float32)
    for n in range(SLOTS // 2):
        row = neighbour_row(neighbours, leaf, pl.program_id(1) * (SLOTS // 2) + n)
        wide = wide + mm16(vectors[row], high_tiles[0, n, 0])
        narrow = narrow + mm16(vectors[row, :ROWS, :], low_tiles[0, n, 0])
    value = NEAR_WEIGHT * (wide[:ROWS] + wide[ROWS:] + narrow)

    @pl.when(pl.program_id(1) == 0)
    def first():
        out[...] = value

    @pl.when(pl.program_id(1) > 0)
    def later():
        out[...] += value


def near_again(neighbours, vectors, tiles, box):
    half = (1, SLOTS // 2, 1, LEAF, LEAF)
    high = pl.BlockSpec(half, lambda a, h: (a, h, 0, 0, 0))
    low = pl.BlockSpec(half, lambda a, h: (a, h, 1, 0, 0))
    return pl.pallas_call(
        again_body,
        grid=(OWN, 2),
        out_shape=(shape(ROWS, OWN * LEAF), shape(*box.shape)),
        in_specs=[SMEM, VMEM, high, low, VMEM],
        out_specs=[pl.BlockSpec((ROWS, LEAF), lambda a, h: (0, a)), VMEM],
        compiler_params=params(40),
        cost_estimate=cost(6_000_000_000, 30_000_000),
        name="near_again",
    )(neighbours, vectors, tiles, tiles, box)


def box_local(maps, boxes):
    g = lax.axis_index("gx")
    row = jnp.concatenate(
        [boxes[jnp.bitwise_xor(g, m)] for m in range(1, BOX_SPAN + 1)], axis=1
    )
    return mm(row, maps[...])


def cell_local(couplings, cell_transfer, received):
    local = mm(unpacked_rows(received[:, 0, 0:128]), cell_transfer[0], NT)
    for s in range(LIST):
        low = 128 * (s + 1)
        local = local + mm(
            unpacked_rows(received[:, 0, low : low + 128]), couplings[0, s], NT
        )
    return local


def middle_body(
    couplings, cell_transfer, lifts, vector, near, received, image, message, moment, dots
):
    local = cell_local(couplings, cell_transfer, received)
    total = jnp.zeros((ROWS, RANK), jnp.float32)
    sums = [jnp.zeros((ROWS, 1), jnp.float32)] * 3
    for a in range(OWN):
        part = slice(a * LEAF, (a + 1) * LEAF)
        lift = lifts[:, part]
        value = vector[:, part]
        result = value + near[:, part] + mm(local, lift)
        image[:, part] = result
        total = total + mm(result, lift, NT)
        for k, product in enumerate((value * value, value * result, result * result)):
            sums[k] = sums[k] + jnp.sum(product, axis=1, keepdims=True)
    send_moments(message, total, cell_transfer[0])
    moment[...] = total
    lane = lax.broadcasted_iota(jnp.int32, (ROWS, 128), 1)
    table = jnp.zeros((ROWS, 128), jnp.float32)
    for k, column in enumerate(sums):
        table = jnp.where(lane == k, column, table)
    dots[...] = table


def middle(couplings, cell_transfer, lifts, vector, near, received):
    return pl.pallas_call(
        middle_body,
        out_shape=(shape(ROWS, OWN * LEAF), shape(GROUP, 1, 256), shape(ROWS, RANK), shape(ROWS, 128)),
        in_specs=[VMEM] * 6,
        out_specs=[VMEM] * 4,
        compiler_params=params(),
        cost_estimate=cost(80_000_000, 3_000_000),
        name="middle",
    )(couplings, cell_transfer, lifts, vector, near, received)


def finish_body(cell_transfer, lifts, local, near, vector, first, received, iterate, residual):
    expansion = local[...] + mm(
        unpacked_rows(received[:, 0, 256:384]), cell_transfer[0], NT
    )
    table = jnp.sum(received[:, 0, 0:256], axis=0, keepdims=True)
    table = jnp.concatenate([table, jnp.zeros((7, 256), jnp.float32)], axis=0).T
    norm = table[:ROWS, 0:1]
    lean = table[ROWS : 2 * ROWS, 0:1]
    square = table[2 * ROWS : 3 * ROWS, 0:1]
    cubic = table[3 * ROWS :, 0:1]
    alpha0 = norm / lean
    norm1 = alpha0 * (alpha0 * square - lean)
    beta = norm1 / norm
    grow = 1.0 + beta
    curve = grow * (grow * lean - 2.0 * alpha0 * square) + alpha0 * alpha0 * cubic
    alpha1 = norm1 / curve
    both = alpha0 + alpha1 * grow
    cross = alpha1 * alpha0
    for a in range(OWN):
        part = slice(a * LEAF, (a + 1) * LEAF)
        start = vector[:, part]
        image = first[:, part]
        second = image + near[:, part] + mm(expansion, lifts[:, part])
        iterate[:, part] = both * start - cross * image
        residual[:, part] = start - both * image + cross * second


def finish(cell_transfer, lifts, local, near, vector, first, received):
    return pl.pallas_call(
        finish_body,
        out_shape=(shape(ROWS, OWN * LEAF), shape(ROWS, OWN * LEAF)),
        in_specs=[VMEM] * 7,
        out_specs=[VMEM] * 2,
        compiler_params=params(),
        cost_estimate=cost(20_000_000, 3_000_000),
        name="finish",
    )(cell_transfer, lifts, local, near, vector, first, received)


def exchange(block, axis, mask):
    count = lax.axis_size(axis)
    return lax.ppermute(block, axis, [(i, i ^ mask) for i in range(count)])


def turn(block, axis):
    return lax.all_to_all(block, axis, 0, 0, tiled=True)


def shards(
    points,
    targets,
    basis,
    leaf_transfer,
    cell_transfer,
    box_parent_transfer,
    cell_coupling,
    box_coupling,
    top_coupling,
    neighbours,
    cell_lists,
):
    lifts, message, targets, points = up(
        basis, leaf_transfer, cell_transfer, cell_lists, targets, points
    )
    partner_points = exchange(points, "gy", 1)
    partner_targets = exchange(targets, "gy", 1)
    maps = coarse(box_parent_transfer, box_coupling, top_coupling)
    left, right = features(points, partner_points)
    vectors = joined(targets, partner_targets)
    tiles, near = near_tiles(neighbours, left, right, vectors)
    box, picked, lists = route(turn(message, "gy"))
    message = boxes(turn(box, "gx"), maps, picked)
    first, message, moment, dots = middle(
        cell_coupling, cell_transfer, lifts, targets, near, turn(message, "gy")
    )

    partner_first = exchange(first, "gy", 1)
    box, picked = route(turn(message, "gy"), lists)
    picked = turn(picked, "gy")
    near, box = near_again(neighbours, joined(first, partner_first), tiles, box)
    local, chunk, sums = tally(
        cell_coupling, maps, moment, dots, first, near, picked, turn(box, "gx")
    )
    message = turn(spread(turn(sums, "gx"), chunk), "gy")
    return finish(cell_transfer, lifts, local, near, targets, first, message)


def solution(mesh):
    both = ("gx", "gy")
    return jax.shard_map(
        shards,
        mesh=mesh,
        in_specs=(
            P(None, both),
            P(None, both),
            P(both, None, None),
            P(both, None, None),
            P(both, None, None),
            P(),
            P(both, None, None, None),
            P(),
            P(),
            P(both, None),
            P(both, None),
        ),
        out_specs=(P(None, both), P(None, both)),
        check_vma=False,
    )
```

```python
import functools
import math

import jax
import jax.numpy as jnp
from jax import lax
from jax.experimental import pallas as pl
from jax.experimental.pallas import tpu as pltpu
from jax.sharding import PartitionSpec as P

RANK = 64
ROWS = 64
LEAF = 512
OWN = 4
SLOTS = 6
FEATURES = 32
BOX_SPAN = 9
GROUP = 32
LIST = 4

UNIT = 2.0 * math.sqrt(3.0)
NEAR_WEIGHT = 0.0625

EXACT = lax.Precision.HIGHEST
VMEM = pl.BlockSpec(memory_space=pltpu.VMEM)
SMEM = pl.BlockSpec(memory_space=pltpu.SMEM)
ANY = pl.BlockSpec(memory_space=pl.ANY)

NN = (((1,), (0,)), ((), ()))
NT = (((1,), (1,)), ((), ()))
TN = (((0,), (0,)), ((), ()))


def mm(a, b, dims=NN):
    return lax.dot_general(a, b, dims, precision=EXACT, preferred_element_type=jnp.float32)


def mm16(a, b, dims=NN):
    return lax.dot_general(a, b, dims, preferred_element_type=jnp.float32)


def split2(value):
    high = value.astype(jnp.bfloat16)
    return high, (value - high.astype(jnp.float32)).astype(jnp.bfloat16)


def split3(value):
    first = value.astype(jnp.bfloat16).astype(jnp.float32)
    rest = value - first
    second = rest.astype(jnp.bfloat16).astype(jnp.float32)
    return first, second, rest - second


def params(mib=32):
    return pltpu.CompilerParams(vmem_limit_bytes=mib * 1024 * 1024)


def cost(flops, moved, special=0):
    return pl.CostEstimate(flops=flops, bytes_accessed=moved, transcendentals=special)


def shape(*dims, dtype=jnp.float32):
    return jax.ShapeDtypeStruct(dims, dtype)


def packed_rows(table):
    return jnp.concatenate([table[: ROWS // 2], table[ROWS // 2 :]], axis=1)


def unpacked_rows(table):
    return jnp.concatenate([table[:, :RANK], table[:, RANK:]], axis=0)


def fetch(pairs, sems):
    copies = [
        pltpu.make_async_copy(source, target, sems.at[k])
        for k, (source, target) in enumerate(pairs)
    ]
    for copy in copies:
        copy.start()
    return copies


def send_moments(message, moment, cell_transfer):
    message[:, 0, 0:128] = packed_rows(moment)
    message[:, 0, 128:256] = packed_rows(mm(moment, cell_transfer))


def up_body(
    basis, leaf_transfer, cell_transfer, lists, vector, points, lifts, message, v, p, b, t, c, sems
):
    copies = fetch(
        (
            (leaf_transfer, t),
            (basis, b),
            (vector, v),
            (cell_transfer, c),
            (points, p),
        ),
        sems,
    )
    for copy in copies:
        copy.wait()
    total = jnp.zeros((ROWS, RANK), jnp.float32)
    for a in range(OWN):
        lift = mm(t[a], b[a], TN)
        lifts[:, a * LEAF : (a + 1) * LEAF] = lift
        total = total + mm(v[:, a * LEAF : (a + 1) * LEAF], lift, NT)
    send_moments(message, total, c[0])
    lane = lax.broadcasted_iota(jnp.int32, (GROUP, 128), 1)
    table = jnp.zeros((GROUP, 128), jnp.int32)
    for k in range(LIST):
        table = jnp.where(lane == k, lists[0, k] & (GROUP - 1), table)
    message[:, 0, 256:384] = table.astype(jnp.float32)


def up(basis, leaf_transfer, cell_transfer, cell_lists, vector, points):
    return pl.pallas_call(
        up_body,
        out_shape=(
            shape(RANK, OWN * LEAF),
            shape(GROUP, 1, 384),
            shape(ROWS, OWN * LEAF),
            shape(3, OWN * LEAF),
        ),
        in_specs=[ANY] * 3 + [SMEM, ANY, ANY],
        out_specs=[VMEM] * 4,
        scratch_shapes=[
            pltpu.VMEM((OWN, RANK, LEAF), jnp.float32),
            pltpu.VMEM((OWN, RANK, RANK), jnp.float32),
            pltpu.VMEM((1, RANK, RANK), jnp.float32),
            pltpu.SemaphoreType.DMA((5,)),
        ],
        compiler_params=params(60),
        cost_estimate=cost(60_000_000, 2_000_000),
        name="up",
    )(basis, leaf_transfer, cell_transfer, cell_lists, vector, points)


def coarse_body(parent_ref, box_ref, top_ref, out, parent, box_coupling, top_coupling, sems):
    g = lax.axis_index("gx")
    t = g // 2
    copies = fetch(
        (
            (parent_ref, parent),
            (box_ref.at[g], box_coupling),
            (top_ref.at[t], top_coupling),
        ),
        sems,
    )
    out[...] = jnp.zeros_like(out)
    for copy in copies:
        copy.wait()
    for m in range(1, BOX_SPAN + 1):
        if m >= 2:
            if m % 2 == 0:
                through = mm(parent[g], top_coupling[m // 2 - 1])
            value = mm(parent[jnp.bitwise_xor(g, m)], through, NT)
        if m <= 3:
            direct = box_coupling[m - 1].T
            value = direct if m == 1 else value + direct
        low = (m - 1) * 128
        out[low : low + 64, 0:64] = value
        out[low + 64 : low + 128, 64:128] = value


def coarse(parent, box_coupling, top_coupling):
    return pl.pallas_call(
        coarse_body,
        out_shape=shape(BOX_SPAN * 128, 128),
        in_specs=[ANY] * 3,
        out_specs=VMEM,
        scratch_shapes=[
            pltpu.VMEM((16, RANK, RANK), jnp.float32),
            pltpu.VMEM((3, RANK, RANK), jnp.float32),
            pltpu.VMEM((4, RANK, RANK), jnp.float32),
            pltpu.SemaphoreType.DMA((3,)),
        ],
        compiler_params=params(60),
        cost_estimate=cost(50_000_000, 2_000_000),
        name="coarse",
    )(parent, box_coupling, top_coupling)


def route_body(with_lists, received, *refs):
    chunk = jnp.sum(received[:, 0, 128:256], axis=0, keepdims=True)
    cells = received[:, 0, 0:128]
    if with_lists:
        box, picked, lists = refs[-3:]
        numbers = received[:, 0, 256:384]
        lists[...] = numbers
    else:
        box, picked = refs[-2:]
        numbers = refs[0][...]
    box[...] = jnp.broadcast_to(chunk[None], box.shape)
    member = lax.broadcasted_iota(jnp.int32, (GROUP, GROUP), 1).astype(jnp.float32)
    for s in range(LIST):
        chooser = (numbers[:, s : s + 1] == member).astype(jnp.float32)
        picked[:, 0, s * 128 : (s + 1) * 128] = mm(chooser, cells)


def route(received, lists, after):
    outs = (shape(16 if lists is None else 1, 1, 128), shape(GROUP, 1, LIST * 128))
    operands = (received,) + (() if lists is None else (lists,))
    if lists is None:
        outs = outs + (shape(GROUP, 128),)
    return pl.pallas_call(
        functools.partial(route_body, lists is None),
        out_shape=outs,
        in_specs=[VMEM] * len(operands) + [ANY] * len(after),
        out_specs=[VMEM] * len(outs),
        compiler_params=params(8),
        cost_estimate=cost(4_000_000, 200_000),
        name="route",
    )(*operands, *after)


def boxes_body(received, maps, picked, message):
    g = lax.axis_index("gx")
    row = jnp.concatenate(
        [received[jnp.bitwise_xor(g, m)] for m in range(1, BOX_SPAN + 1)], axis=1
    )
    local = mm(row, maps[...])
    message[:, 0, 0:128] = jnp.broadcast_to(local, (GROUP, 128))
    message[:, 0, 128:640] = picked[:, 0, :]


def boxes(received, maps, picked):
    return pl.pallas_call(
        boxes_body,
        out_shape=shape(GROUP, 1, 640),
        in_specs=[VMEM] * 3,
        out_specs=VMEM,
        compiler_params=params(),
        cost_estimate=cost(4_000_000, 200_000),
        name="boxes",
    )(received, maps, picked)


def sum_rows(columns):
    lane = lax.broadcasted_iota(jnp.int32, (ROWS, 128), 1)
    table = jnp.zeros((ROWS, 128), jnp.float32)
    for k, column in columns:
        table = jnp.where(lane == k, column, table)
    table = table.T
    upper = jnp.concatenate([table[0:1], table[1:2]], axis=1)
    lower = jnp.concatenate([table[2:3], table[3:4]], axis=1)
    return jnp.concatenate([upper, lower], axis=0)


def tally_body(
    couplings,
    maps,
    moment,
    dots,
    image,
    near0,
    near1,
    picked,
    own,
    one,
    two,
    four,
    eight,
    local,
    chunk,
    sums,
):
    expansion = jnp.zeros((ROWS, RANK), jnp.float32)
    for k in range(LIST):
        part = unpacked_rows(picked[:, 0, k * 128 : (k + 1) * 128])
        expansion = expansion + mm(part, couplings[0, k], NT)
    local[...] = expansion
    square = dots[:, 2:3]
    cubic = square + jnp.sum(moment[...] * expansion, axis=1, keepdims=True)
    for a in range(OWN):
        part = slice(a * LEAF, (a + 1) * LEAF)
        near = near_of(near0, near1, a)
        cubic = cubic + jnp.sum(image[:, part] * near, axis=1, keepdims=True)
    rows = sum_rows(((0, dots[:, 0:1]), (1, dots[:, 1:2]), (2, square), (3, cubic)))
    others = [ref[k] for ref in (one, two, four, eight) for k in range(ref.shape[0])]
    row = mm(jnp.concatenate(others, axis=1), maps[...])
    chunk[...] = row
    product = row * own[0]
    place = lax.broadcasted_iota(jnp.int32, (2, 128), 0) * 128
    place = place + lax.broadcasted_iota(jnp.int32, (2, 128), 1)
    column = 128 + RANK + lax.axis_index("gy")
    for half in range(2):
        term = jnp.sum(product[:, half * RANK : (half + 1) * RANK], axis=1, keepdims=True)
        rows = rows + jnp.where(place == column + half * (ROWS // 2), term, 0.0)
    sums[...] = jnp.broadcast_to(rows[None], sums.shape)


def tally(couplings, maps, moment, dots, image, near0, near1, picked, boxes):
    return pl.pallas_call(
        tally_body,
        out_shape=(shape(ROWS, RANK), shape(1, 128), shape(16, 2, 128)),
        in_specs=[VMEM] * 13,
        out_specs=[VMEM] * 3,
        compiler_params=params(),
        cost_estimate=cost(4_000_000, 2_500_000),
        name="tally",
    )(couplings, maps, moment, dots, image, near0, near1, picked, *boxes)


def spread_body(received, chunk, message):
    total = jnp.sum(received[...], axis=0)
    message[:, 0, 0:128] = jnp.broadcast_to(total[0:1], (GROUP, 128))
    message[:, 0, 128:256] = jnp.broadcast_to(total[1:2], (GROUP, 128))
    message[:, 0, 256:384] = jnp.broadcast_to(chunk[...], (GROUP, 128))


def spread(received, chunk):
    return pl.pallas_call(
        spread_body,
        out_shape=shape(GROUP, 1, 384),
        in_specs=[VMEM] * 2,
        out_specs=VMEM,
        compiler_params=params(),
        cost_estimate=cost(10_000, 50_000),
        name="spread",
    )(received, chunk)


def features_body(own, partner, left, right, rows):
    block = lax.axis_index("gx") * (lax.axis_size("gy") // 2) + lax.axis_index("gy") // 2
    axis_id = lax.broadcasted_iota(jnp.int32, (3, OWN * LEAF), 0)
    centre = jnp.zeros((3, OWN * LEAF), jnp.int32)
    for axis in range(3):
        place = 1
        for depth in range(1, 11):
            place = place + ((block >> (3 * (depth - 1) + axis)) & 1) * (1 << depth)
        centre = jnp.where(axis_id == axis, place, centre)
    centre = centre.astype(jnp.float32)
    ones = jnp.ones((3, OWN * LEAF), jnp.float32)
    for half, source in enumerate((own, partner)):
        local = (source[...] - centre) * UNIT
        one, two, three = split3(local)
        square = jnp.sum(local * local, axis=0, keepdims=True)
        squares = split3(square)
        rows[24:32, :] = jnp.zeros((8, OWN * LEAF), jnp.float32)
        for place, piece in enumerate((one, one, two, one, two, three)):
            rows[3 * place : 3 * place + 3, :] = -2.0 * piece
        for place, piece in enumerate(squares):
            rows[18 + place : 19 + place, :] = piece
        rows[21:24, :] = ones
        for a in range(OWN):
            left[half * OWN + a] = rows[:, a * LEAF : (a + 1) * LEAF].T.astype(jnp.bfloat16)
        if half == 0:
            for place, piece in enumerate((one, two, one, three, two, one)):
                rows[3 * place : 3 * place + 3, :] = piece
            rows[18:21, :] = ones
            for place, piece in enumerate(squares):
                rows[21 + place : 22 + place, :] = piece
            for a in range(OWN):
                right[a] = rows[:, a * LEAF : (a + 1) * LEAF].astype(jnp.bfloat16)


def features(own, partner):
    return pl.pallas_call(
        features_body,
        out_shape=(
            shape(2 * OWN, LEAF, FEATURES, dtype=jnp.bfloat16),
            shape(OWN, FEATURES, LEAF, dtype=jnp.bfloat16),
        ),
        in_specs=[VMEM] * 2,
        out_specs=[VMEM] * 2,
        scratch_shapes=[pltpu.VMEM((FEATURES, OWN * LEAF), jnp.float32)],
        compiler_params=params(),
        cost_estimate=cost(1_000_000, 400_000),
        name="features",
    )(own, partner)


def joined_body(own, partner, out):
    for half, source in enumerate((own, partner)):
        for a in range(OWN):
            high, low = split2(source[:, a * LEAF : (a + 1) * LEAF])
            out[half * OWN + a, :ROWS, :] = high
            out[half * OWN + a, ROWS:, :] = low


def joined(own, partner):
    return pl.pallas_call(
        joined_body,
        out_shape=shape(2 * OWN, 2 * ROWS, LEAF, dtype=jnp.bfloat16),
        in_specs=[VMEM] * 2,
        out_specs=VMEM,
        compiler_params=params(),
        cost_estimate=cost(1_000_000, 2_000_000),
        name="joined",
    )(own, partner)


def neighbour_row(neighbours, leaf, n):
    parity = lax.axis_index("gy") % 2
    return jnp.bitwise_xor(neighbours[leaf, n] & (2 * OWN - 1), OWN * parity)


def tiles_body(first_leaf, neighbours, left, right, vectors, *refs):
    tiles, out, square = refs[-3:]
    leaf = pl.program_id(0) + first_leaf
    target = right[leaf]
    rows = [neighbour_row(neighbours, leaf, n) for n in range(SLOTS)]
    wide = jnp.zeros((2 * ROWS, LEAF), jnp.float32)
    narrow = jnp.zeros((ROWS, LEAF), jnp.float32)
    step = 32

    def measure(n):
        square[n % 2] = mm16(left[rows[n]], target)

    def apply(n, wide, narrow):
        wide = wide + mm16(vectors[rows[n]], tiles[0, n, 0])
        narrow = narrow + mm16(vectors[rows[n], :ROWS, :], tiles[0, n, 1])
        return wide, narrow

    measure(0)
    for n in range(SLOTS):
        if n + 1 < SLOTS:
            measure(n + 1)
        if n > 0:
            wide, narrow = apply(n - 1, wide, narrow)
        for low in range(0, LEAF, step):
            part = jnp.maximum(square[n % 2, low : low + step, :], 1e-12)
            u = part * lax.rsqrt(part)
            kernel = jnp.exp(-u) * (1.0 + u)
            high, rest = split2(kernel)
            tiles[0, n, 0, low : low + step, :] = high
            tiles[0, n, 1, low : low + step, :] = rest
    wide, narrow = apply(SLOTS - 1, wide, narrow)
    out[...] = NEAR_WEIGHT * (wide[:ROWS] + wide[ROWS:] + narrow)


def near_tiles(leaves, neighbours, left, right, vectors, after=()):
    tile = shape(len(leaves), SLOTS, 2, LEAF, LEAF, dtype=jnp.bfloat16)
    block = pl.BlockSpec((1, SLOTS, 2, LEAF, LEAF), lambda a: (a, 0, 0, 0, 0))
    return pl.pallas_call(
        functools.partial(tiles_body, leaves[0]),
        grid=(len(leaves),),
        out_shape=(tile, shape(ROWS, len(leaves) * LEAF)),
        in_specs=[SMEM] + [VMEM] * 3 + [ANY] * len(after),
        out_specs=[block, pl.BlockSpec((ROWS, LEAF), lambda a: (0, a))],
        scratch_shapes=[pltpu.VMEM((2, LEAF, LEAF), jnp.float32)],
        compiler_params=params(40),
        cost_estimate=cost(
            2_000_000_000 * len(leaves), 7_000_000 * len(leaves), 3_000_000 * len(leaves)
        ),
        name="near_tiles",
    )(neighbours, left, right, vectors, *after)


def again_body(first_leaf, neighbours, vectors, high_tiles, low_tiles, out):
    leaf = pl.program_id(0) + first_leaf
    wide = jnp.zeros((2 * ROWS, LEAF), jnp.float32)
    narrow = jnp.zeros((ROWS, LEAF), jnp.float32)
    for n in range(SLOTS // 2):
        row = neighbour_row(neighbours, leaf, pl.program_id(1) * (SLOTS // 2) + n)
        wide = wide + mm16(vectors[row], high_tiles[0, n, 0])
        narrow = narrow + mm16(vectors[row, :ROWS, :], low_tiles[0, n, 0])
    value = NEAR_WEIGHT * (wide[:ROWS] + wide[ROWS:] + narrow)

    @pl.when(pl.program_id(1) == 0)
    def first():
        out[...] = value

    @pl.when(pl.program_id(1) > 0)
    def later():
        out[...] += value


def near_again(leaves, neighbours, vectors, tiles):
    half = (1, SLOTS // 2, 1, LEAF, LEAF)
    high = pl.BlockSpec(half, lambda a, h: (a, h, 0, 0, 0))
    low = pl.BlockSpec(half, lambda a, h: (a, h, 1, 0, 0))
    return pl.pallas_call(
        functools.partial(again_body, leaves[0]),
        grid=(len(leaves), 2),
        out_shape=shape(ROWS, len(leaves) * LEAF),
        in_specs=[SMEM, VMEM, high, low],
        out_specs=pl.BlockSpec((ROWS, LEAF), lambda a, h: (0, a)),
        compiler_params=params(40),
        cost_estimate=cost(1_500_000_000 * len(leaves), 7_000_000 * len(leaves)),
        name="near_again",
    )(neighbours, vectors, tiles, tiles)


def near_of(near0, near1, a):
    return near0[...] if a == 0 else near1[:, (a - 1) * LEAF : a * LEAF]


def cell_local(couplings, cell_transfer, received):
    local = mm(unpacked_rows(received[:, 0, 0:128]), cell_transfer[0], NT)
    for s in range(LIST):
        low = 128 * (s + 1)
        local = local + mm(
            unpacked_rows(received[:, 0, low : low + 128]), couplings[0, s], NT
        )
    return local


def middle_body(
    couplings, cell_transfer, lifts, vector, near0, near1, received, image, message, moment, dots
):
    local = cell_local(couplings, cell_transfer, received)
    total = jnp.zeros((ROWS, RANK), jnp.float32)
    sums = [jnp.zeros((ROWS, 1), jnp.float32)] * 3
    for a in range(OWN):
        part = slice(a * LEAF, (a + 1) * LEAF)
        lift = lifts[:, part]
        value = vector[:, part]
        result = value + near_of(near0, near1, a) + mm(local, lift)
        image[:, part] = result
        total = total + mm(result, lift, NT)
        for k, product in enumerate((value * value, value * result, result * result)):
            sums[k] = sums[k] + jnp.sum(product, axis=1, keepdims=True)
    send_moments(message, total, cell_transfer[0])
    moment[...] = total
    lane = lax.broadcasted_iota(jnp.int32, (ROWS, 128), 1)
    table = jnp.zeros((ROWS, 128), jnp.float32)
    for k, column in enumerate(sums):
        table = jnp.where(lane == k, column, table)
    dots[...] = table


def middle(couplings, cell_transfer, lifts, vector, near0, near1, received):
    return pl.pallas_call(
        middle_body,
        out_shape=(shape(ROWS, OWN * LEAF), shape(GROUP, 1, 256), shape(ROWS, RANK), shape(ROWS, 128)),
        in_specs=[VMEM] * 7,
        out_specs=[VMEM] * 4,
        compiler_params=params(),
        cost_estimate=cost(80_000_000, 3_000_000),
        name="middle",
    )(couplings, cell_transfer, lifts, vector, near0, near1, received)


def finish_body(
    cell_transfer, lifts, local, near0, near1, vector, first, received, iterate, residual
):
    expansion = local[...] + mm(
        unpacked_rows(received[:, 0, 256:384]), cell_transfer[0], NT
    )
    table = jnp.sum(received[:, 0, 0:256], axis=0, keepdims=True)
    table = jnp.concatenate([table, jnp.zeros((7, 256), jnp.float32)], axis=0).T
    norm = table[:ROWS, 0:1]
    lean = table[ROWS : 2 * ROWS, 0:1]
    square = table[2 * ROWS : 3 * ROWS, 0:1]
    cubic = table[3 * ROWS :, 0:1]
    alpha0 = norm / lean
    norm1 = alpha0 * (alpha0 * square - lean)
    beta = norm1 / norm
    grow = 1.0 + beta
    curve = grow * (grow * lean - 2.0 * alpha0 * square) + alpha0 * alpha0 * cubic
    alpha1 = norm1 / curve
    both = alpha0 + alpha1 * grow
    cross = alpha1 * alpha0
    for a in range(OWN):
        part = slice(a * LEAF, (a + 1) * LEAF)
        start = vector[:, part]
        image = first[:, part]
        near = near_of(near0, near1, a)
        second = image + near + mm(expansion, lifts[:, part])
        iterate[:, part] = both * start - cross * image
        residual[:, part] = start - both * image + cross * second


def finish(cell_transfer, lifts, local, near0, near1, vector, first, received):
    return pl.pallas_call(
        finish_body,
        out_shape=(shape(ROWS, OWN * LEAF), shape(ROWS, OWN * LEAF)),
        in_specs=[VMEM] * 8,
        out_specs=[VMEM] * 2,
        compiler_params=params(),
        cost_estimate=cost(20_000_000, 3_000_000),
        name="finish",
    )(cell_transfer, lifts, local, near0, near1, vector, first, received)


def exchange(block, axis, mask):
    count = lax.axis_size(axis)
    return lax.ppermute(block, axis, [(i, i ^ mask) for i in range(count)])


def turn(block, axis):
    return lax.all_to_all(block, axis, 0, 0, tiled=True)


def shards(
    points,
    targets,
    basis,
    leaf_transfer,
    cell_transfer,
    box_parent_transfer,
    cell_coupling,
    box_coupling,
    top_coupling,
    neighbours,
    cell_lists,
):
    lifts, message, targets, points = up(
        basis, leaf_transfer, cell_transfer, cell_lists, targets, points
    )
    partner_points = exchange(points, "gy", 1)
    partner_targets = exchange(targets, "gy", 1)
    maps = coarse(box_parent_transfer, box_coupling, top_coupling)
    left, right = features(points, partner_points)
    vectors = joined(targets, partner_targets)
    tiles0, near0 = near_tiles((0,), neighbours, left, right, vectors)
    box, picked, lists = route(turn(message, "gy"), None, (near0,))
    message = boxes(turn(box, "gx"), maps, picked)
    tiles1, near1 = near_tiles((1, 2, 3), neighbours, left, right, vectors, (message,))
    first, message, moment, dots = middle(
        cell_coupling, cell_transfer, lifts, targets, near0, near1, turn(message, "gy")
    )

    partner_first = exchange(first, "gy", 1)
    vectors = joined(first, partner_first)
    near1 = near_again((1, 2, 3), neighbours, vectors, tiles1)
    box, picked = route(turn(message, "gy"), lists, (near1,))
    picked = turn(picked, "gy")
    near0 = near_again((0,), neighbours, vectors, tiles0)
    one = exchange(box, "gx", 1)
    pair = jnp.concatenate([box, one], axis=0)
    two = exchange(pair, "gx", 2)
    eight = exchange(pair, "gx", 8)
    four = exchange(jnp.concatenate([pair, two], axis=0), "gx", 4)
    local, chunk, sums = tally(
        cell_coupling,
        maps,
        moment,
        dots,
        first,
        near0,
        near1,
        picked,
        (box, one, two, four, eight),
    )
    message = turn(spread(turn(sums, "gx"), chunk), "gy")
    return finish(cell_transfer, lifts, local, near0, near1, targets, first, message)


def solution(mesh):
    both = ("gx", "gy")
    return jax.shard_map(
        shards,
        mesh=mesh,
        in_specs=(
            P(None, both),
            P(None, both),
            P(both, None, None),
            P(both, None, None),
            P(both, None, None),
            P(),
            P(both, None, None, None),
            P(),
            P(),
            P(both, None),
            P(both, None),
        ),
        out_specs=(P(None, both), P(None, both)),
        check_vma=False,
    )
```

```python
import functools
import math

import jax
import jax.numpy as jnp
from jax import lax
from jax.experimental import pallas as pl
from jax.experimental.pallas import tpu as pltpu
from jax.sharding import PartitionSpec as P

RANK = 64
ROWS = 64
LEAF = 512
OWN = 4
SLOTS = 6
FEATURES = 32
BOX_SPAN = 9
GROUP = 32
LIST = 4

UNIT = 2.0 * math.sqrt(3.0)
NEAR_WEIGHT = 0.0625

EXACT = lax.Precision.HIGHEST
VMEM = pl.BlockSpec(memory_space=pltpu.VMEM)
SMEM = pl.BlockSpec(memory_space=pltpu.SMEM)
ANY = pl.BlockSpec(memory_space=pl.ANY)

NN = (((1,), (0,)), ((), ()))
NT = (((1,), (1,)), ((), ()))
TN = (((0,), (0,)), ((), ()))


def mm(a, b, dims=NN):
    return lax.dot_general(a, b, dims, precision=EXACT, preferred_element_type=jnp.float32)


def mm16(a, b, dims=NN):
    return lax.dot_general(a, b, dims, preferred_element_type=jnp.float32)


def split2(value):
    high = value.astype(jnp.bfloat16)
    return high, (value - high.astype(jnp.float32)).astype(jnp.bfloat16)


def split3(value):
    first = value.astype(jnp.bfloat16).astype(jnp.float32)
    rest = value - first
    second = rest.astype(jnp.bfloat16).astype(jnp.float32)
    return first, second, rest - second


def params(mib=32):
    return pltpu.CompilerParams(vmem_limit_bytes=mib * 1024 * 1024)


def cost(flops, moved, special=0):
    return pl.CostEstimate(flops=flops, bytes_accessed=moved, transcendentals=special)


def shape(*dims, dtype=jnp.float32):
    return jax.ShapeDtypeStruct(dims, dtype)


def packed_rows(table):
    return jnp.concatenate([table[: ROWS // 2], table[ROWS // 2 :]], axis=1)


def unpacked_rows(table):
    return jnp.concatenate([table[:, :RANK], table[:, RANK:]], axis=0)


def fetch(pairs, sems):
    copies = [
        pltpu.make_async_copy(source, target, sems.at[k])
        for k, (source, target) in enumerate(pairs)
    ]
    for copy in copies:
        copy.start()
    return copies


def send_moments(message, moment, cell_transfer):
    message[:, 0, 0:128] = packed_rows(moment)
    message[:, 0, 128:256] = packed_rows(mm(moment, cell_transfer))


def up_body(
    basis, leaf_transfer, cell_transfer, lists, vector, points, lifts, message, v, p, b, t, c, sems
):
    copies = fetch(
        (
            (leaf_transfer, t),
            (basis, b),
            (vector, v),
            (cell_transfer, c),
            (points, p),
        ),
        sems,
    )
    for copy in copies:
        copy.wait()
    total = jnp.zeros((ROWS, RANK), jnp.float32)
    for a in range(OWN):
        lift = mm(t[a], b[a], TN)
        lifts[:, a * LEAF : (a + 1) * LEAF] = lift
        total = total + mm(v[:, a * LEAF : (a + 1) * LEAF], lift, NT)
    send_moments(message, total, c[0])
    lane = lax.broadcasted_iota(jnp.int32, (GROUP, 128), 1)
    table = jnp.zeros((GROUP, 128), jnp.int32)
    for k in range(LIST):
        table = jnp.where(lane == k, lists[0, k] & (GROUP - 1), table)
    message[:, 0, 256:384] = table.astype(jnp.float32)


def up(basis, leaf_transfer, cell_transfer, cell_lists, vector, points):
    return pl.pallas_call(
        up_body,
        out_shape=(
            shape(RANK, OWN * LEAF),
            shape(GROUP, 1, 384),
            shape(ROWS, OWN * LEAF),
            shape(3, OWN * LEAF),
        ),
        in_specs=[ANY] * 3 + [SMEM, ANY, ANY],
        out_specs=[VMEM] * 4,
        scratch_shapes=[
            pltpu.VMEM((OWN, RANK, LEAF), jnp.float32),
            pltpu.VMEM((OWN, RANK, RANK), jnp.float32),
            pltpu.VMEM((1, RANK, RANK), jnp.float32),
            pltpu.SemaphoreType.DMA((5,)),
        ],
        compiler_params=params(60),
        cost_estimate=cost(60_000_000, 2_000_000),
        name="up",
    )(basis, leaf_transfer, cell_transfer, cell_lists, vector, points)


def coarse_body(parent_ref, box_ref, top_ref, out, parent, box_coupling, top_coupling, sems):
    g = lax.axis_index("gx")
    t = g // 2
    copies = fetch(
        (
            (parent_ref, parent),
            (box_ref.at[g], box_coupling),
            (top_ref.at[t], top_coupling),
        ),
        sems,
    )
    out[...] = jnp.zeros_like(out)
    for copy in copies:
        copy.wait()
    for m in range(1, BOX_SPAN + 1):
        if m >= 2:
            if m % 2 == 0:
                through = mm(parent[g], top_coupling[m // 2 - 1])
            value = mm(parent[jnp.bitwise_xor(g, m)], through, NT)
        if m <= 3:
            direct = box_coupling[m - 1].T
            value = direct if m == 1 else value + direct
        low = (m - 1) * 128
        out[low : low + 64, 0:64] = value
        out[low + 64 : low + 128, 64:128] = value


def coarse(parent, box_coupling, top_coupling):
    return pl.pallas_call(
        coarse_body,
        out_shape=shape(BOX_SPAN * 128, 128),
        in_specs=[ANY] * 3,
        out_specs=VMEM,
        scratch_shapes=[
            pltpu.VMEM((16, RANK, RANK), jnp.float32),
            pltpu.VMEM((3, RANK, RANK), jnp.float32),
            pltpu.VMEM((4, RANK, RANK), jnp.float32),
            pltpu.SemaphoreType.DMA((3,)),
        ],
        compiler_params=params(60),
        cost_estimate=cost(50_000_000, 2_000_000),
        name="coarse",
    )(parent, box_coupling, top_coupling)


def route_body(with_lists, received, *refs):
    chunk = jnp.sum(received[:, 0, 128:256], axis=0, keepdims=True)
    cells = received[:, 0, 0:128]
    if with_lists:
        box, picked, lists = refs[-3:]
        numbers = received[:, 0, 256:384]
        lists[...] = numbers
    else:
        box, picked = refs[-2:]
        numbers = refs[0][...]
    box[...] = jnp.broadcast_to(chunk[None], box.shape)
    member = lax.broadcasted_iota(jnp.int32, (GROUP, GROUP), 1).astype(jnp.float32)
    for s in range(LIST):
        chooser = (numbers[:, s : s + 1] == member).astype(jnp.float32)
        picked[:, 0, s * 128 : (s + 1) * 128] = mm(chooser, cells)


def route(received, lists, after):
    outs = (shape(16 if lists is None else 1, 1, 128), shape(GROUP, 1, LIST * 128))
    operands = (received,) + (() if lists is None else (lists,))
    if lists is None:
        outs = outs + (shape(GROUP, 128),)
    return pl.pallas_call(
        functools.partial(route_body, lists is None),
        out_shape=outs,
        in_specs=[VMEM] * len(operands) + [ANY] * len(after),
        out_specs=[VMEM] * len(outs),
        compiler_params=params(8),
        cost_estimate=cost(4_000_000, 200_000),
        name="route",
    )(*operands, *after)


def boxes_body(received, maps, picked, message):
    g = lax.axis_index("gx")
    row = jnp.concatenate(
        [received[jnp.bitwise_xor(g, m)] for m in range(1, BOX_SPAN + 1)], axis=1
    )
    local = mm(row, maps[...])
    message[:, 0, 0:128] = jnp.broadcast_to(local, (GROUP, 128))
    message[:, 0, 128:640] = picked[:, 0, :]


def boxes(received, maps, picked):
    return pl.pallas_call(
        boxes_body,
        out_shape=shape(GROUP, 1, 640),
        in_specs=[VMEM] * 3,
        out_specs=VMEM,
        compiler_params=params(),
        cost_estimate=cost(4_000_000, 200_000),
        name="boxes",
    )(received, maps, picked)


def sum_rows(columns):
    lane = lax.broadcasted_iota(jnp.int32, (ROWS, 128), 1)
    table = jnp.zeros((ROWS, 128), jnp.float32)
    for k, column in columns:
        table = jnp.where(lane == k, column, table)
    table = table.T
    upper = jnp.concatenate([table[0:1], table[1:2]], axis=1)
    lower = jnp.concatenate([table[2:3], table[3:4]], axis=1)
    return jnp.concatenate([upper, lower], axis=0)


def tally_body(
    couplings,
    maps,
    moment,
    dots,
    image,
    near,
    picked,
    own,
    one,
    two,
    four,
    eight,
    local,
    chunk,
    sums,
):
    expansion = jnp.zeros((ROWS, RANK), jnp.float32)
    for k in range(LIST):
        part = unpacked_rows(picked[:, 0, k * 128 : (k + 1) * 128])
        expansion = expansion + mm(part, couplings[0, k], NT)
    local[...] = expansion
    square = dots[:, 2:3]
    cubic = square + jnp.sum(moment[...] * expansion, axis=1, keepdims=True)
    for a in range(OWN):
        part = slice(a * LEAF, (a + 1) * LEAF)
        cubic = cubic + jnp.sum(image[:, part] * near[:, part], axis=1, keepdims=True)
    rows = sum_rows(((0, dots[:, 0:1]), (1, dots[:, 1:2]), (2, square), (3, cubic)))
    others = [ref[k] for ref in (one, two, four, eight) for k in range(ref.shape[0])]
    row = mm(jnp.concatenate(others, axis=1), maps[...])
    chunk[...] = row
    product = row * own[0]
    place = lax.broadcasted_iota(jnp.int32, (2, 128), 0) * 128
    place = place + lax.broadcasted_iota(jnp.int32, (2, 128), 1)
    column = 128 + RANK + lax.axis_index("gy")
    for half in range(2):
        term = jnp.sum(product[:, half * RANK : (half + 1) * RANK], axis=1, keepdims=True)
        rows = rows + jnp.where(place == column + half * (ROWS // 2), term, 0.0)
    sums[...] = jnp.broadcast_to(rows[None], sums.shape)


def tally(couplings, maps, moment, dots, image, near, picked, boxes):
    return pl.pallas_call(
        tally_body,
        out_shape=(shape(ROWS, RANK), shape(1, 128), shape(16, 2, 128)),
        in_specs=[VMEM] * 12,
        out_specs=[VMEM] * 3,
        compiler_params=params(),
        cost_estimate=cost(4_000_000, 2_500_000),
        name="tally",
    )(couplings, maps, moment, dots, image, near, picked, *boxes)


def spread_body(received, chunk, message):
    total = jnp.sum(received[...], axis=0)
    message[:, 0, 0:128] = jnp.broadcast_to(total[0:1], (GROUP, 128))
    message[:, 0, 128:256] = jnp.broadcast_to(total[1:2], (GROUP, 128))
    message[:, 0, 256:384] = jnp.broadcast_to(chunk[...], (GROUP, 128))


def spread(received, chunk):
    return pl.pallas_call(
        spread_body,
        out_shape=shape(GROUP, 1, 384),
        in_specs=[VMEM] * 2,
        out_specs=VMEM,
        compiler_params=params(),
        cost_estimate=cost(10_000, 50_000),
        name="spread",
    )(received, chunk)


def features_body(own, partner, left, right, rows):
    block = lax.axis_index("gx") * (lax.axis_size("gy") // 2) + lax.axis_index("gy") // 2
    axis_id = lax.broadcasted_iota(jnp.int32, (3, OWN * LEAF), 0)
    centre = jnp.zeros((3, OWN * LEAF), jnp.int32)
    for axis in range(3):
        place = 1
        for depth in range(1, 11):
            place = place + ((block >> (3 * (depth - 1) + axis)) & 1) * (1 << depth)
        centre = jnp.where(axis_id == axis, place, centre)
    centre = centre.astype(jnp.float32)
    ones = jnp.ones((3, OWN * LEAF), jnp.float32)
    for half, source in enumerate((own, partner)):
        local = (source[...] - centre) * UNIT
        one, two, three = split3(local)
        square = jnp.sum(local * local, axis=0, keepdims=True)
        squares = split3(square)
        rows[24:32, :] = jnp.zeros((8, OWN * LEAF), jnp.float32)
        for place, piece in enumerate((one, one, two, one, two, three)):
            rows[3 * place : 3 * place + 3, :] = -2.0 * piece
        for place, piece in enumerate(squares):
            rows[18 + place : 19 + place, :] = piece
        rows[21:24, :] = ones
        for a in range(OWN):
            left[half * OWN + a] = rows[:, a * LEAF : (a + 1) * LEAF].T.astype(jnp.bfloat16)
        if half == 0:
            for place, piece in enumerate((one, two, one, three, two, one)):
                rows[3 * place : 3 * place + 3, :] = piece
            rows[18:21, :] = ones
            for place, piece in enumerate(squares):
                rows[21 + place : 22 + place, :] = piece
            for a in range(OWN):
                right[a] = rows[:, a * LEAF : (a + 1) * LEAF].astype(jnp.bfloat16)


def features(own, partner):
    return pl.pallas_call(
        features_body,
        out_shape=(
            shape(2 * OWN, LEAF, FEATURES, dtype=jnp.bfloat16),
            shape(OWN, FEATURES, LEAF, dtype=jnp.bfloat16),
        ),
        in_specs=[VMEM] * 2,
        out_specs=[VMEM] * 2,
        scratch_shapes=[pltpu.VMEM((FEATURES, OWN * LEAF), jnp.float32)],
        compiler_params=params(),
        cost_estimate=cost(1_000_000, 400_000),
        name="features",
    )(own, partner)


def joined_body(own, partner, out):
    for half, source in enumerate((own, partner)):
        for a in range(OWN):
            high, low = split2(source[:, a * LEAF : (a + 1) * LEAF])
            out[half * OWN + a, :ROWS, :] = high
            out[half * OWN + a, ROWS:, :] = low


def joined(own, partner):
    return pl.pallas_call(
        joined_body,
        out_shape=shape(2 * OWN, 2 * ROWS, LEAF, dtype=jnp.bfloat16),
        in_specs=[VMEM] * 2,
        out_specs=VMEM,
        compiler_params=params(),
        cost_estimate=cost(1_000_000, 2_000_000),
        name="joined",
    )(own, partner)


def neighbour_row(neighbours, leaf, n):
    parity = lax.axis_index("gy") % 2
    return jnp.bitwise_xor(neighbours[leaf, n] & (2 * OWN - 1), OWN * parity)


def tiles_body(first_leaf, neighbours, left, right, vectors, *refs):
    tiles, out, square = refs[-3:]
    leaf = pl.program_id(0) + first_leaf
    target = right[leaf]
    rows = [neighbour_row(neighbours, leaf, n) for n in range(SLOTS)]
    wide = jnp.zeros((2 * ROWS, LEAF), jnp.float32)
    narrow = jnp.zeros((ROWS, LEAF), jnp.float32)
    step = 32

    def measure(n):
        square[n % 2] = mm16(left[rows[n]], target)

    def apply(n, wide, narrow):
        wide = wide + mm16(vectors[rows[n]], tiles[0, n, 0])
        narrow = narrow + mm16(vectors[rows[n], :ROWS, :], tiles[0, n, 1])
        return wide, narrow

    measure(0)
    for n in range(SLOTS):
        if n + 1 < SLOTS:
            measure(n + 1)
        if n > 0:
            wide, narrow = apply(n - 1, wide, narrow)
        for low in range(0, LEAF, step):
            part = jnp.maximum(square[n % 2, low : low + step, :], 1e-12)
            u = part * lax.rsqrt(part)
            kernel = jnp.exp(-u) * (1.0 + u)
            high, rest = split2(kernel)
            tiles[0, n, 0, low : low + step, :] = high
            tiles[0, n, 1, low : low + step, :] = rest
    wide, narrow = apply(SLOTS - 1, wide, narrow)
    out[...] = NEAR_WEIGHT * (wide[:ROWS] + wide[ROWS:] + narrow)


def near_tiles(leaves, neighbours, left, right, vectors, after=()):
    tile = shape(len(leaves), SLOTS, 2, LEAF, LEAF, dtype=jnp.bfloat16)
    block = pl.BlockSpec((1, SLOTS, 2, LEAF, LEAF), lambda a: (a, 0, 0, 0, 0))
    return pl.pallas_call(
        functools.partial(tiles_body, leaves[0]),
        grid=(len(leaves),),
        out_shape=(tile, shape(ROWS, len(leaves) * LEAF)),
        in_specs=[SMEM] + [VMEM] * 3 + [ANY] * len(after),
        out_specs=[block, pl.BlockSpec((ROWS, LEAF), lambda a: (0, a))],
        scratch_shapes=[pltpu.VMEM((2, LEAF, LEAF), jnp.float32)],
        compiler_params=params(40),
        cost_estimate=cost(
            2_000_000_000 * len(leaves), 7_000_000 * len(leaves), 3_000_000 * len(leaves)
        ),
        name="near_tiles",
    )(neighbours, left, right, vectors, *after)


def again_body(first_leaf, neighbours, vectors, high_tiles, low_tiles, out):
    leaf = pl.program_id(0) + first_leaf
    wide = jnp.zeros((2 * ROWS, LEAF), jnp.float32)
    narrow = jnp.zeros((ROWS, LEAF), jnp.float32)
    for n in range(SLOTS // 2):
        row = neighbour_row(neighbours, leaf, pl.program_id(1) * (SLOTS // 2) + n)
        wide = wide + mm16(vectors[row], high_tiles[0, n, 0])
        narrow = narrow + mm16(vectors[row, :ROWS, :], low_tiles[0, n, 0])
    value = NEAR_WEIGHT * (wide[:ROWS] + wide[ROWS:] + narrow)

    @pl.when(pl.program_id(1) == 0)
    def first():
        out[...] = value

    @pl.when(pl.program_id(1) > 0)
    def later():
        out[...] += value


def near_again(leaves, neighbours, vectors, tiles):
    half = (1, SLOTS // 2, 1, LEAF, LEAF)
    high = pl.BlockSpec(half, lambda a, h: (a, h, 0, 0, 0))
    low = pl.BlockSpec(half, lambda a, h: (a, h, 1, 0, 0))
    return pl.pallas_call(
        functools.partial(again_body, leaves[0]),
        grid=(len(leaves), 2),
        out_shape=shape(ROWS, len(leaves) * LEAF),
        in_specs=[SMEM, VMEM, high, low],
        out_specs=pl.BlockSpec((ROWS, LEAF), lambda a, h: (0, a)),
        compiler_params=params(40),
        cost_estimate=cost(1_500_000_000 * len(leaves), 7_000_000 * len(leaves)),
        name="near_again",
    )(neighbours, vectors, tiles, tiles)


def cell_local(couplings, cell_transfer, received):
    local = mm(unpacked_rows(received[:, 0, 0:128]), cell_transfer[0], NT)
    for s in range(LIST):
        low = 128 * (s + 1)
        local = local + mm(
            unpacked_rows(received[:, 0, low : low + 128]), couplings[0, s], NT
        )
    return local


def middle_body(
    couplings, cell_transfer, lifts, vector, near, received, image, message, moment, dots
):
    local = cell_local(couplings, cell_transfer, received)
    total = jnp.zeros((ROWS, RANK), jnp.float32)
    sums = [jnp.zeros((ROWS, 1), jnp.float32)] * 3
    for a in range(OWN):
        part = slice(a * LEAF, (a + 1) * LEAF)
        lift = lifts[:, part]
        value = vector[:, part]
        result = value + near[:, part] + mm(local, lift)
        image[:, part] = result
        total = total + mm(result, lift, NT)
        for k, product in enumerate((value * value, value * result, result * result)):
            sums[k] = sums[k] + jnp.sum(product, axis=1, keepdims=True)
    send_moments(message, total, cell_transfer[0])
    moment[...] = total
    lane = lax.broadcasted_iota(jnp.int32, (ROWS, 128), 1)
    table = jnp.zeros((ROWS, 128), jnp.float32)
    for k, column in enumerate(sums):
        table = jnp.where(lane == k, column, table)
    dots[...] = table


def middle(couplings, cell_transfer, lifts, vector, near, received):
    return pl.pallas_call(
        middle_body,
        out_shape=(shape(ROWS, OWN * LEAF), shape(GROUP, 1, 256), shape(ROWS, RANK), shape(ROWS, 128)),
        in_specs=[VMEM] * 6,
        out_specs=[VMEM] * 4,
        compiler_params=params(),
        cost_estimate=cost(80_000_000, 3_000_000),
        name="middle",
    )(couplings, cell_transfer, lifts, vector, near, received)


def finish_body(
    cell_transfer, lifts, local, near, vector, first, received, iterate, residual
):
    expansion = local[...] + mm(
        unpacked_rows(received[:, 0, 256:384]), cell_transfer[0], NT
    )
    table = jnp.sum(received[:, 0, 0:256], axis=0, keepdims=True)
    table = jnp.concatenate([table, jnp.zeros((7, 256), jnp.float32)], axis=0).T
    norm = table[:ROWS, 0:1]
    lean = table[ROWS : 2 * ROWS, 0:1]
    square = table[2 * ROWS : 3 * ROWS, 0:1]
    cubic = table[3 * ROWS :, 0:1]
    alpha0 = norm / lean
    norm1 = alpha0 * (alpha0 * square - lean)
    beta = norm1 / norm
    grow = 1.0 + beta
    curve = grow * (grow * lean - 2.0 * alpha0 * square) + alpha0 * alpha0 * cubic
    alpha1 = norm1 / curve
    both = alpha0 + alpha1 * grow
    cross = alpha1 * alpha0
    for a in range(OWN):
        part = slice(a * LEAF, (a + 1) * LEAF)
        start = vector[:, part]
        image = first[:, part]
        second = image + near[:, part] + mm(expansion, lifts[:, part])
        iterate[:, part] = both * start - cross * image
        residual[:, part] = start - both * image + cross * second


def finish(cell_transfer, lifts, local, near, vector, first, received):
    return pl.pallas_call(
        finish_body,
        out_shape=(shape(ROWS, OWN * LEAF), shape(ROWS, OWN * LEAF)),
        in_specs=[VMEM] * 7,
        out_specs=[VMEM] * 2,
        compiler_params=params(),
        cost_estimate=cost(20_000_000, 3_000_000),
        name="finish",
    )(cell_transfer, lifts, local, near, vector, first, received)


def exchange(block, axis, mask):
    count = lax.axis_size(axis)
    return lax.ppermute(block, axis, [(i, i ^ mask) for i in range(count)])


def turn(block, axis):
    return lax.all_to_all(block, axis, 0, 0, tiled=True)


def shards(
    points,
    targets,
    basis,
    leaf_transfer,
    cell_transfer,
    box_parent_transfer,
    cell_coupling,
    box_coupling,
    top_coupling,
    neighbours,
    cell_lists,
):
    lifts, message, targets, points = up(
        basis, leaf_transfer, cell_transfer, cell_lists, targets, points
    )
    partner_points = exchange(points, "gy", 1)
    partner_targets = exchange(targets, "gy", 1)
    maps = coarse(box_parent_transfer, box_coupling, top_coupling)
    left, right = features(points, partner_points)
    vectors = joined(targets, partner_targets)
    tiles, near = near_tiles(range(OWN), neighbours, left, right, vectors)
    box, picked, lists = route(turn(message, "gy"), None, ())
    message = boxes(turn(box, "gx"), maps, picked)
    first, message, moment, dots = middle(
        cell_coupling, cell_transfer, lifts, targets, near, turn(message, "gy")
    )

    partner_first = exchange(first, "gy", 1)
    near = near_again(range(OWN), neighbours, joined(first, partner_first), tiles)
    box, picked = route(turn(message, "gy"), lists, (near,))
    picked = turn(picked, "gy")
    one = exchange(box, "gx", 1)
    pair = jnp.concatenate([box, one], axis=0)
    two = exchange(pair, "gx", 2)
    eight = exchange(pair, "gx", 8)
    four = exchange(jnp.concatenate([pair, two], axis=0), "gx", 4)
    local, chunk, sums = tally(
        cell_coupling,
        maps,
        moment,
        dots,
        first,
        near,
        picked,
        (box, one, two, four, eight),
    )
    message = turn(spread(turn(sums, "gx"), chunk), "gy")
    return finish(cell_transfer, lifts, local, near, targets, first, message)


def solution(mesh):
    both = ("gx", "gy")
    return jax.shard_map(
        shards,
        mesh=mesh,
        in_specs=(
            P(None, both),
            P(None, both),
            P(both, None, None),
            P(both, None, None),
            P(both, None, None),
            P(),
            P(both, None, None, None),
            P(),
            P(),
            P(both, None),
            P(both, None),
        ),
        out_specs=(P(None, both), P(None, both)),
        check_vma=False,
    )
```

```python
import functools
import math

import jax
import jax.numpy as jnp
from jax import lax
from jax.experimental import pallas as pl
from jax.experimental.pallas import tpu as pltpu
from jax.sharding import PartitionSpec as P

RANK = 64
ROWS = 64
LEAF = 512
OWN = 4
SLOTS = 6
FEATURES = 32
BOX_SPAN = 9
GROUP = 32
LIST = 4

UNIT = 2.0 * math.sqrt(3.0)
NEAR_WEIGHT = 0.0625

EXACT = lax.Precision.HIGHEST
VMEM = pl.BlockSpec(memory_space=pltpu.VMEM)
SMEM = pl.BlockSpec(memory_space=pltpu.SMEM)
ANY = pl.BlockSpec(memory_space=pl.ANY)

NN = (((1,), (0,)), ((), ()))
NT = (((1,), (1,)), ((), ()))
TN = (((0,), (0,)), ((), ()))


def mm_row(a, b, dims=NN):
    return lax.dot_general(a, b, dims, precision=EXACT, preferred_element_type=jnp.float32)


def mm16(a, b, dims=NN):
    return lax.dot_general(a, b, dims, preferred_element_type=jnp.float32)


def split2(value):
    high = value.astype(jnp.bfloat16)
    return high, (value - high.astype(jnp.float32)).astype(jnp.bfloat16)


def mm(a, b, dims=NN):
    a_high, a_low = split2(a)
    b_high, b_low = split2(b)
    small = mm16(a_high, b_low, dims) + mm16(a_low, b_high, dims)
    return mm16(a_high, b_high, dims) + small


def split3(value):
    first = value.astype(jnp.bfloat16).astype(jnp.float32)
    rest = value - first
    second = rest.astype(jnp.bfloat16).astype(jnp.float32)
    return first, second, rest - second


def params(mib=32):
    return pltpu.CompilerParams(vmem_limit_bytes=mib * 1024 * 1024)


def cost(flops, moved, special=0):
    return pl.CostEstimate(flops=flops, bytes_accessed=moved, transcendentals=special)


def shape(*dims, dtype=jnp.float32):
    return jax.ShapeDtypeStruct(dims, dtype)


def packed_rows(table):
    return jnp.concatenate([table[: ROWS // 2], table[ROWS // 2 :]], axis=1)


def unpacked_rows(table):
    return jnp.concatenate([table[:, :RANK], table[:, RANK:]], axis=0)


def fetch(pairs, sems):
    copies = [
        pltpu.make_async_copy(source, target, sems.at[k])
        for k, (source, target) in enumerate(pairs)
    ]
    for copy in copies:
        copy.start()
    return copies


def send_moments(message, moment, cell_transfer):
    message[:, 0, 0:128] = packed_rows(moment)
    message[:, 0, 128:256] = packed_rows(mm(moment, cell_transfer))


def up_body(
    basis, leaf_transfer, cell_transfer, lists, vector, points, lifts, message, v, p, b, t, c, sems
):
    copies = fetch(
        (
            (leaf_transfer, t),
            (basis, b),
            (vector, v),
            (cell_transfer, c),
            (points, p),
        ),
        sems,
    )
    for copy in copies:
        copy.wait()
    total = jnp.zeros((ROWS, RANK), jnp.float32)
    for a in range(OWN):
        lift = mm(t[a], b[a], TN)
        lifts[:, a * LEAF : (a + 1) * LEAF] = lift
        total = total + mm(v[:, a * LEAF : (a + 1) * LEAF], lift, NT)
    send_moments(message, total, c[0])
    lane = lax.broadcasted_iota(jnp.int32, (GROUP, 128), 1)
    table = jnp.zeros((GROUP, 128), jnp.int32)
    for k in range(LIST):
        table = jnp.where(lane == k, lists[0, k] & (GROUP - 1), table)
    message[:, 0, 256:384] = table.astype(jnp.float32)


def up(basis, leaf_transfer, cell_transfer, cell_lists, vector, points):
    return pl.pallas_call(
        up_body,
        out_shape=(
            shape(RANK, OWN * LEAF),
            shape(GROUP, 1, 384),
            shape(ROWS, OWN * LEAF),
            shape(3, OWN * LEAF),
        ),
        in_specs=[ANY] * 3 + [SMEM, ANY, ANY],
        out_specs=[VMEM] * 4,
        scratch_shapes=[
            pltpu.VMEM((OWN, RANK, LEAF), jnp.float32),
            pltpu.VMEM((OWN, RANK, RANK), jnp.float32),
            pltpu.VMEM((1, RANK, RANK), jnp.float32),
            pltpu.SemaphoreType.DMA((5,)),
        ],
        compiler_params=params(60),
        cost_estimate=cost(60_000_000, 2_000_000),
        name="up",
    )(basis, leaf_transfer, cell_transfer, cell_lists, vector, points)


def coarse_body(parent_ref, box_ref, top_ref, out, parent, box_coupling, top_coupling, sems):
    g = lax.axis_index("gx")
    t = g // 2
    copies = fetch(
        (
            (parent_ref, parent),
            (box_ref.at[g], box_coupling),
            (top_ref.at[t], top_coupling),
        ),
        sems,
    )
    out[...] = jnp.zeros_like(out)
    for copy in copies:
        copy.wait()
    for m in range(1, BOX_SPAN + 1):
        if m >= 2:
            if m % 2 == 0:
                through = mm(parent[g], top_coupling[m // 2 - 1])
            value = mm(parent[jnp.bitwise_xor(g, m)], through, NT)
        if m <= 3:
            direct = box_coupling[m - 1].T
            value = direct if m == 1 else value + direct
        low = (m - 1) * 128
        out[low : low + 64, 0:64] = value
        out[low + 64 : low + 128, 64:128] = value


def coarse(parent, box_coupling, top_coupling):
    return pl.pallas_call(
        coarse_body,
        out_shape=shape(BOX_SPAN * 128, 128),
        in_specs=[ANY] * 3,
        out_specs=VMEM,
        scratch_shapes=[
            pltpu.VMEM((16, RANK, RANK), jnp.float32),
            pltpu.VMEM((3, RANK, RANK), jnp.float32),
            pltpu.VMEM((4, RANK, RANK), jnp.float32),
            pltpu.SemaphoreType.DMA((3,)),
        ],
        compiler_params=params(60),
        cost_estimate=cost(50_000_000, 2_000_000),
        name="coarse",
    )(parent, box_coupling, top_coupling)


def route_body(with_lists, received, lists, *outs):
    box, picked = outs[0], outs[1]
    chunk = jnp.sum(received[:, 0, 128:256], axis=0, keepdims=True)
    box[...] = jnp.broadcast_to(chunk[None], box.shape)
    cells = received[:, 0, 0:128]
    numbers = received[:, 0, 256:384] if with_lists else lists[...]
    member = lax.broadcasted_iota(jnp.int32, (GROUP, GROUP), 1).astype(jnp.float32)
    for s in range(LIST):
        chooser = (numbers[:, s : s + 1] == member).astype(jnp.float32)
        picked[:, 0, s * 128 : (s + 1) * 128] = mm(chooser, cells)
    if with_lists:
        outs[2][...] = numbers


def route(received, lists=None):
    first = lists is None
    outs = (shape(16, 1, 128), shape(GROUP, 1, LIST * 128))
    if first:
        body = lambda received, *outs: route_body(True, received, None, *outs)
        outs = outs + (shape(GROUP, 128),)
        operands = (received,)
    else:
        body = functools.partial(route_body, False)
        operands = (received, lists)
    return pl.pallas_call(
        body,
        out_shape=outs,
        in_specs=[VMEM] * len(operands),
        out_specs=[VMEM] * len(outs),
        compiler_params=params(),
        cost_estimate=cost(4_000_000, 200_000),
        name="route",
    )(*operands)


def boxes_body(received, maps, picked, message):
    g = lax.axis_index("gx")
    row = jnp.concatenate(
        [received[jnp.bitwise_xor(g, m)] for m in range(1, BOX_SPAN + 1)], axis=1
    )
    local = mm_row(row, maps[...])
    message[:, 0, 0:128] = jnp.broadcast_to(local, (GROUP, 128))
    message[:, 0, 128:640] = picked[:, 0, :]


def boxes(received, maps, picked):
    return pl.pallas_call(
        boxes_body,
        out_shape=shape(GROUP, 1, 640),
        in_specs=[VMEM] * 3,
        out_specs=VMEM,
        compiler_params=params(),
        cost_estimate=cost(4_000_000, 200_000),
        name="boxes",
    )(received, maps, picked)


def sum_rows(columns):
    lane = lax.broadcasted_iota(jnp.int32, (ROWS, 128), 1)
    table = jnp.zeros((ROWS, 128), jnp.float32)
    for k, column in columns:
        table = jnp.where(lane == k, column, table)
    table = table.T
    upper = jnp.concatenate([table[0:1], table[1:2]], axis=1)
    lower = jnp.concatenate([table[2:3], table[3:4]], axis=1)
    return jnp.concatenate([upper, lower], axis=0)


def tally_body(
    couplings, maps, moment, dots, image, near, picked, received, local, chunk, sums
):
    expansion = jnp.zeros((ROWS, RANK), jnp.float32)
    for k in range(LIST):
        part = unpacked_rows(picked[:, 0, k * 128 : (k + 1) * 128])
        expansion = expansion + mm(part, couplings[0, k], NT)
    local[...] = expansion
    square = dots[:, 2:3]
    cubic = square + jnp.sum(moment[...] * expansion, axis=1, keepdims=True)
    for a in range(OWN):
        part = slice(a * LEAF, (a + 1) * LEAF)
        cubic = cubic + jnp.sum(image[:, part] * near[:, part], axis=1, keepdims=True)
    rows = sum_rows(((0, dots[:, 0:1]), (1, dots[:, 1:2]), (2, square), (3, cubic)))
    row = box_local(maps, received)
    chunk[...] = row
    product = row * received[lax.axis_index("gx")]
    place = lax.broadcasted_iota(jnp.int32, (2, 128), 0) * 128
    place = place + lax.broadcasted_iota(jnp.int32, (2, 128), 1)
    column = 128 + RANK + lax.axis_index("gy")
    for half in range(2):
        term = jnp.sum(product[:, half * RANK : (half + 1) * RANK], axis=1, keepdims=True)
        rows = rows + jnp.where(place == column + half * (ROWS // 2), term, 0.0)
    sums[...] = jnp.broadcast_to(rows[None], sums.shape)


def tally(couplings, maps, moment, dots, image, near, picked, received):
    return pl.pallas_call(
        tally_body,
        out_shape=(shape(ROWS, RANK), shape(1, 128), shape(16, 2, 128)),
        in_specs=[VMEM] * 8,
        out_specs=[VMEM] * 3,
        compiler_params=params(),
        cost_estimate=cost(4_000_000, 2_500_000),
        name="tally",
    )(couplings, maps, moment, dots, image, near, picked, received)


def spread_body(received, chunk, message):
    total = jnp.sum(received[...], axis=0)
    message[:, 0, 0:128] = jnp.broadcast_to(total[0:1], (GROUP, 128))
    message[:, 0, 128:256] = jnp.broadcast_to(total[1:2], (GROUP, 128))
    message[:, 0, 256:384] = jnp.broadcast_to(chunk[...], (GROUP, 128))


def spread(received, chunk):
    return pl.pallas_call(
        spread_body,
        out_shape=shape(GROUP, 1, 384),
        in_specs=[VMEM] * 2,
        out_specs=VMEM,
        compiler_params=params(),
        cost_estimate=cost(10_000, 50_000),
        name="spread",
    )(received, chunk)


def features_body(own, partner, left, right, rows):
    block = lax.axis_index("gx") * (lax.axis_size("gy") // 2) + lax.axis_index("gy") // 2
    axis_id = lax.broadcasted_iota(jnp.int32, (3, OWN * LEAF), 0)
    centre = jnp.zeros((3, OWN * LEAF), jnp.int32)
    for axis in range(3):
        place = 1
        for depth in range(1, 11):
            place = place + ((block >> (3 * (depth - 1) + axis)) & 1) * (1 << depth)
        centre = jnp.where(axis_id == axis, place, centre)
    centre = centre.astype(jnp.float32)
    ones = jnp.ones((3, OWN * LEAF), jnp.float32)
    for half, source in enumerate((own, partner)):
        local = (source[...] - centre) * UNIT
        one, two, three = split3(local)
        square = jnp.sum(local * local, axis=0, keepdims=True)
        squares = split3(square)
        rows[24:32, :] = jnp.zeros((8, OWN * LEAF), jnp.float32)
        for place, piece in enumerate((one, one, two, one, two, three)):
            rows[3 * place : 3 * place + 3, :] = -2.0 * piece
        for place, piece in enumerate(squares):
            rows[18 + place : 19 + place, :] = piece
        rows[21:24, :] = ones
        for a in range(OWN):
            left[half * OWN + a] = rows[:, a * LEAF : (a + 1) * LEAF].T.astype(jnp.bfloat16)
        if half == 0:
            for place, piece in enumerate((one, two, one, three, two, one)):
                rows[3 * place : 3 * place + 3, :] = piece
            rows[18:21, :] = ones
            for place, piece in enumerate(squares):
                rows[21 + place : 22 + place, :] = piece
            for a in range(OWN):
                right[a] = rows[:, a * LEAF : (a + 1) * LEAF].astype(jnp.bfloat16)


def features(own, partner):
    return pl.pallas_call(
        features_body,
        out_shape=(
            shape(2 * OWN, LEAF, FEATURES, dtype=jnp.bfloat16),
            shape(OWN, FEATURES, LEAF, dtype=jnp.bfloat16),
        ),
        in_specs=[VMEM] * 2,
        out_specs=[VMEM] * 2,
        scratch_shapes=[pltpu.VMEM((FEATURES, OWN * LEAF), jnp.float32)],
        compiler_params=params(),
        cost_estimate=cost(1_000_000, 400_000),
        name="features",
    )(own, partner)


def joined_body(own, partner, out):
    for half, source in enumerate((own, partner)):
        for a in range(OWN):
            high, low = split2(source[:, a * LEAF : (a + 1) * LEAF])
            out[half * OWN + a, :ROWS, :] = high
            out[half * OWN + a, ROWS:, :] = low


def joined(own, partner):
    return pl.pallas_call(
        joined_body,
        out_shape=shape(2 * OWN, 2 * ROWS, LEAF, dtype=jnp.bfloat16),
        in_specs=[VMEM] * 2,
        out_specs=VMEM,
        compiler_params=params(),
        cost_estimate=cost(1_000_000, 2_000_000),
        name="joined",
    )(own, partner)


def neighbour_row(neighbours, leaf, n):
    parity = lax.axis_index("gy") % 2
    return jnp.bitwise_xor(neighbours[leaf, n] & (2 * OWN - 1), OWN * parity)


def tiles_body(neighbours, left, right, vectors, tiles, out, square):
    leaf = pl.program_id(0)
    target = right[leaf]
    rows = [neighbour_row(neighbours, leaf, n) for n in range(SLOTS)]
    wide = jnp.zeros((2 * ROWS, LEAF), jnp.float32)
    narrow = jnp.zeros((ROWS, LEAF), jnp.float32)
    step = 32

    def measure(n):
        square[n % 2] = mm16(left[rows[n]], target)

    def apply(n, wide, narrow):
        wide = wide + mm16(vectors[rows[n]], tiles[0, n, 0])
        narrow = narrow + mm16(vectors[rows[n], :ROWS, :], tiles[0, n, 1])
        return wide, narrow

    measure(0)
    for n in range(SLOTS):
        if n + 1 < SLOTS:
            measure(n + 1)
        if n > 0:
            wide, narrow = apply(n - 1, wide, narrow)
        for low in range(0, LEAF, step):
            part = jnp.maximum(square[n % 2, low : low + step, :], 1e-12)
            u = part * lax.rsqrt(part)
            kernel = jnp.exp(-u) * (1.0 + u)
            high, rest = split2(kernel)
            tiles[0, n, 0, low : low + step, :] = high
            tiles[0, n, 1, low : low + step, :] = rest
    wide, narrow = apply(SLOTS - 1, wide, narrow)
    out[...] = NEAR_WEIGHT * (wide[:ROWS] + wide[ROWS:] + narrow)


def near_tiles(neighbours, left, right, vectors):
    tile = shape(OWN, SLOTS, 2, LEAF, LEAF, dtype=jnp.bfloat16)
    block = pl.BlockSpec((1, SLOTS, 2, LEAF, LEAF), lambda a: (a, 0, 0, 0, 0))
    return pl.pallas_call(
        tiles_body,
        grid=(OWN,),
        out_shape=(tile, shape(ROWS, OWN * LEAF)),
        in_specs=[SMEM] + [VMEM] * 3,
        out_specs=[block, pl.BlockSpec((ROWS, LEAF), lambda a: (0, a))],
        scratch_shapes=[pltpu.VMEM((2, LEAF, LEAF), jnp.float32)],
        compiler_params=params(40),
        cost_estimate=cost(8_000_000_000, 30_000_000, 12_000_000),
        name="near_tiles",
    )(neighbours, left, right, vectors)


def again_body(neighbours, vectors, high_tiles, low_tiles, box, out, box_out):
    box_out[...] = box[...]
    leaf = pl.program_id(0)
    wide = jnp.zeros((2 * ROWS, LEAF), jnp.float32)
    narrow = jnp.zeros((ROWS, LEAF), jnp.float32)
    for n in range(SLOTS // 2):
        row = neighbour_row(neighbours, leaf, pl.program_id(1) * (SLOTS // 2) + n)
        wide = wide + mm16(vectors[row], high_tiles[0, n, 0])
        narrow = narrow + mm16(vectors[row, :ROWS, :], low_tiles[0, n, 0])
    value = NEAR_WEIGHT * (wide[:ROWS] + wide[ROWS:] + narrow)

    @pl.when(pl.program_id(1) == 0)
    def first():
        out[...] = value

    @pl.when(pl.program_id(1) > 0)
    def later():
        out[...] += value


def near_again(neighbours, vectors, tiles, box):
    half = (1, SLOTS // 2, 1, LEAF, LEAF)
    high = pl.BlockSpec(half, lambda a, h: (a, h, 0, 0, 0))
    low = pl.BlockSpec(half, lambda a, h: (a, h, 1, 0, 0))
    return pl.pallas_call(
        again_body,
        grid=(OWN, 2),
        out_shape=(shape(ROWS, OWN * LEAF), shape(*box.shape)),
        in_specs=[SMEM, VMEM, high, low, VMEM],
        out_specs=[pl.BlockSpec((ROWS, LEAF), lambda a, h: (0, a)), VMEM],
        compiler_params=params(40),
        cost_estimate=cost(6_000_000_000, 30_000_000),
        name="near_again",
    )(neighbours, vectors, tiles, tiles, box)


def box_local(maps, boxes):
    g = lax.axis_index("gx")
    row = jnp.concatenate(
        [boxes[jnp.bitwise_xor(g, m)] for m in range(1, BOX_SPAN + 1)], axis=1
    )
    return mm_row(row, maps[...])


def cell_local(couplings, cell_transfer, received):
    local = mm(unpacked_rows(received[:, 0, 0:128]), cell_transfer[0], NT)
    for s in range(LIST):
        low = 128 * (s + 1)
        local = local + mm(
            unpacked_rows(received[:, 0, low : low + 128]), couplings[0, s], NT
        )
    return local


def middle_body(
    couplings, cell_transfer, lifts, vector, near, received, image, message, moment, dots
):
    local = cell_local(couplings, cell_transfer, received)
    total = jnp.zeros((ROWS, RANK), jnp.float32)
    sums = [jnp.zeros((ROWS, 1), jnp.float32)] * 3
    for a in range(OWN):
        part = slice(a * LEAF, (a + 1) * LEAF)
        lift = lifts[:, part]
        value = vector[:, part]
        result = value + near[:, part] + mm(local, lift)
        image[:, part] = result
        total = total + mm(result, lift, NT)
        for k, product in enumerate((value * value, value * result, result * result)):
            sums[k] = sums[k] + jnp.sum(product, axis=1, keepdims=True)
    send_moments(message, total, cell_transfer[0])
    moment[...] = total
    lane = lax.broadcasted_iota(jnp.int32, (ROWS, 128), 1)
    table = jnp.zeros((ROWS, 128), jnp.float32)
    for k, column in enumerate(sums):
        table = jnp.where(lane == k, column, table)
    dots[...] = table


def middle(couplings, cell_transfer, lifts, vector, near, received):
    return pl.pallas_call(
        middle_body,
        out_shape=(shape(ROWS, OWN * LEAF), shape(GROUP, 1, 256), shape(ROWS, RANK), shape(ROWS, 128)),
        in_specs=[VMEM] * 6,
        out_specs=[VMEM] * 4,
        compiler_params=params(),
        cost_estimate=cost(80_000_000, 3_000_000),
        name="middle",
    )(couplings, cell_transfer, lifts, vector, near, received)


def finish_body(cell_transfer, lifts, local, near, vector, first, received, iterate, residual):
    expansion = local[...] + mm(
        unpacked_rows(received[:, 0, 256:384]), cell_transfer[0], NT
    )
    table = jnp.sum(received[:, 0, 0:256], axis=0, keepdims=True)
    table = jnp.concatenate([table, jnp.zeros((7, 256), jnp.float32)], axis=0).T
    norm = table[:ROWS, 0:1]
    lean = table[ROWS : 2 * ROWS, 0:1]
    square = table[2 * ROWS : 3 * ROWS, 0:1]
    cubic = table[3 * ROWS :, 0:1]
    alpha0 = norm / lean
    norm1 = alpha0 * (alpha0 * square - lean)
    beta = norm1 / norm
    grow = 1.0 + beta
    curve = grow * (grow * lean - 2.0 * alpha0 * square) + alpha0 * alpha0 * cubic
    alpha1 = norm1 / curve
    both = alpha0 + alpha1 * grow
    cross = alpha1 * alpha0
    for a in range(OWN):
        part = slice(a * LEAF, (a + 1) * LEAF)
        start = vector[:, part]
        image = first[:, part]
        second = image + near[:, part] + mm(expansion, lifts[:, part])
        iterate[:, part] = both * start - cross * image
        residual[:, part] = start - both * image + cross * second


def finish(cell_transfer, lifts, local, near, vector, first, received):
    return pl.pallas_call(
        finish_body,
        out_shape=(shape(ROWS, OWN * LEAF), shape(ROWS, OWN * LEAF)),
        in_specs=[VMEM] * 7,
        out_specs=[VMEM] * 2,
        compiler_params=params(),
        cost_estimate=cost(20_000_000, 3_000_000),
        name="finish",
    )(cell_transfer, lifts, local, near, vector, first, received)


def exchange(block, axis, mask):
    count = lax.axis_size(axis)
    return lax.ppermute(block, axis, [(i, i ^ mask) for i in range(count)])


def turn(block, axis):
    return lax.all_to_all(block, axis, 0, 0, tiled=True)


def shards(
    points,
    targets,
    basis,
    leaf_transfer,
    cell_transfer,
    box_parent_transfer,
    cell_coupling,
    box_coupling,
    top_coupling,
    neighbours,
    cell_lists,
):
    lifts, message, targets, points = up(
        basis, leaf_transfer, cell_transfer, cell_lists, targets, points
    )
    partner_points = exchange(points, "gy", 1)
    partner_targets = exchange(targets, "gy", 1)
    maps = coarse(box_parent_transfer, box_coupling, top_coupling)
    left, right = features(points, partner_points)
    vectors = joined(targets, partner_targets)
    tiles, near = near_tiles(neighbours, left, right, vectors)
    box, picked, lists = route(turn(message, "gy"))
    message = boxes(turn(box, "gx"), maps, picked)
    first, message, moment, dots = middle(
        cell_coupling, cell_transfer, lifts, targets, near, turn(message, "gy")
    )

    partner_first = exchange(first, "gy", 1)
    box, picked = route(turn(message, "gy"), lists)
    picked = turn(picked, "gy")
    near, box = near_again(neighbours, joined(first, partner_first), tiles, box)
    local, chunk, sums = tally(
        cell_coupling, maps, moment, dots, first, near, picked, turn(box, "gx")
    )
    message = turn(spread(turn(sums, "gx"), chunk), "gy")
    return finish(cell_transfer, lifts, local, near, targets, first, message)


def solution(mesh):
    both = ("gx", "gy")
    return jax.shard_map(
        shards,
        mesh=mesh,
        in_specs=(
            P(None, both),
            P(None, both),
            P(both, None, None),
            P(both, None, None),
            P(both, None, None),
            P(),
            P(both, None, None, None),
            P(),
            P(),
            P(both, None),
            P(both, None),
        ),
        out_specs=(P(None, both), P(None, both)),
        check_vma=False,
    )
```
